128 devices in a mesh: section: 4 (over x_hi, core), seq: 32 (over x_lo, y, z).
Axes of the slice: x: 4 (x_hi: 2, x_lo: 2; x = x_hi * 2 + x_lo), y: 4, z: 4, core: 2. Of those that a mesh axis runs over, the one named last changes fastest.
Arguments:
- acts: bfloat16 [4, 8192, 4096], P('section', 'seq'), may hold values from -6 to 6
- norm_gain: float32 [4, 4096], P('section'), may hold values from 0.1 to 1.9
- w_query: bfloat16 [4, 4096, 2048], P('section'), may hold values from -0.1875 to 0.1875
- section_key_weights: bfloat16 [4, 4096, 512], P('section', 'seq'), may hold values from -0.1875 to 0.1875
- section_value_weights: bfloat16 [4, 4096, 512], P('section', 'seq'), may hold values from -0.09375 to 0.09375
- w_out: bfloat16 [4, 2048, 4096], P('section', None, 'seq'), may hold values from -0.125 to 0.125
Outputs:
- layer_out: bfloat16 [4, 8192, 4096], P('section', 'seq')
The draws below stay inside these ranges and needn't reach their ends.
All inputs are finite; a program needn't handle non-finite values.
Results may differ from the reference program's by a relative error of at most 0.012.
Values may be sent and summed in bfloat16 or wider, within the bound.
No kernel may reach another device: no remote copies, remote signals or barrier semaphores. Data moves between devices by JAX's collectives and lax.ppermute only.
A program may use at most 192 MiB of HBM per device.

```python
import jax
import jax.numpy as jnp
from jax import lax

MODEL_WIDTH = 4096
QUERY_HEAD_TOTAL = 16
KEY_VALUE_HEADS = 4
HEAD_SIZE = 128
RELAY_SECTIONS = 4
DOCUMENT_TOKENS = 8192


def block_levels(rng, dims, shards, least, top_value):
    level, own = 1.0, jax.random.fold_in(rng, 6)
    for dim, shards_of in shards:
        draws = jnp.exp(jax.random.uniform(jax.random.fold_in(own, dim), (shards_of,), jnp.float32, least / len(shards), top_value / len(shards)))
        level = level * jnp.repeat(draws, dims[dim] // shards_of).reshape([-1 if axis == dim else 1 for axis in range(len(dims))])
    return level


def noise(own_key, dims, spread, limit, shards=(), kind=jnp.bfloat16):
    entries = jax.random.normal(own_key, dims, jnp.float32) * spread
    if len(shards) > 0:
        entries = block_levels(own_key, dims, shards, -0.22, 0.18) * entries
    return jnp.clip(entries, min=-limit, max=limit).astype(kind)


def setup_inputs(seed: int = 0) -> dict:
    arg_keys = jax.random.split(jax.random.key(seed), 7)
    acts = noise(arg_keys[0], (RELAY_SECTIONS, DOCUMENT_TOKENS, MODEL_WIDTH), 1.0, 6.0, ((0, 4), (1, 32)))
    norm_gain = jnp.clip(1.0 + 0.18 * jax.random.normal(arg_keys[1], (RELAY_SECTIONS, MODEL_WIDTH), jnp.float32), 0.1, 1.9)
    w_query = noise(arg_keys[2], (RELAY_SECTIONS, MODEL_WIDTH, QUERY_HEAD_TOTAL * HEAD_SIZE), (MODEL_WIDTH // 4) ** -0.5, 0.1875, ((0, 4),))
    section_key_weights = noise(arg_keys[3], (RELAY_SECTIONS, MODEL_WIDTH, KEY_VALUE_HEADS * HEAD_SIZE), (MODEL_WIDTH // 4) ** -0.5, 0.1875, ((0, 4), (1, 32)))
    section_value_weights = noise(arg_keys[4], (RELAY_SECTIONS, MODEL_WIDTH, KEY_VALUE_HEADS * HEAD_SIZE), MODEL_WIDTH ** -0.5, 0.09375, ((0, 4), (1, 32)))
    w_out = noise(arg_keys[5], (RELAY_SECTIONS, QUERY_HEAD_TOTAL * HEAD_SIZE, MODEL_WIDTH), (QUERY_HEAD_TOTAL * HEAD_SIZE) ** -0.5, 0.125, ((0, 4), (2, 32)))
    return {"acts": acts, "norm_gain": norm_gain, "w_query": w_query, "section_key_weights": section_key_weights, "section_value_weights": section_value_weights, "w_out": w_out}


norm_epsilon = 1e-05
rope_base = 500000.0

def rotary_tables(positions, head_width):
    freqs = rope_base ** (-2.0 * jnp.arange(head_width // 2, dtype=jnp.float32) / head_width)
    angles = positions.astype(jnp.float32)[:, None] * freqs[None, :]
    return (jnp.cos(angles)[:, None, :], jnp.sin(angles)[:, None, :])

def apply_rotary(values, cosine_table, sine_table):
    half_width = values.shape[-1] // 2
    first = values[..., :half_width]
    second = values[..., half_width:]
    return jnp.concatenate([first * cosine_table - second * sine_table, second * cosine_table + first * sine_table], axis=-1)

def layer(tokens, gain, query_weight, key_matrix, value_matrix, out_weight):
    floats = tokens.astype(jnp.float32)
    normalized_input = (floats * lax.rsqrt(lax.optimization_barrier(jnp.mean(floats * floats, axis=-1, keepdims=True)) + norm_epsilon) * gain).astype(jnp.bfloat16)
    cosine_table, sine_table = rotary_tables(jnp.arange(DOCUMENT_TOKENS, dtype=jnp.int32), HEAD_SIZE)
    query = apply_rotary(jnp.dot(normalized_input, query_weight, preferred_element_type=jnp.float32).reshape(DOCUMENT_TOKENS, QUERY_HEAD_TOTAL, HEAD_SIZE), cosine_table, sine_table).astype(jnp.bfloat16)
    key = apply_rotary(jnp.dot(normalized_input, key_matrix, preferred_element_type=jnp.float32).reshape(DOCUMENT_TOKENS, KEY_VALUE_HEADS, HEAD_SIZE), cosine_table, sine_table).astype(jnp.bfloat16)
    value_states = jnp.dot(normalized_input, value_matrix, preferred_element_type=jnp.float32).astype(jnp.bfloat16).reshape(DOCUMENT_TOKENS, KEY_VALUE_HEADS, HEAD_SIZE)
    group_width = QUERY_HEAD_TOTAL // KEY_VALUE_HEADS
    score_scale = HEAD_SIZE ** (-0.5)

    def one_head(head_index):
        query_head = lax.dynamic_index_in_dim(query, head_index, 1, keepdims=False)
        key_head = lax.dynamic_index_in_dim(key, head_index // group_width, 1, keepdims=False)
        value_head = lax.dynamic_index_in_dim(value_states, head_index // group_width, 1, keepdims=False)
        scores = jnp.dot(query_head, key_head.T, preferred_element_type=jnp.float32) * score_scale
        exp_scores = jnp.exp(scores)
        softmax_out = (exp_scores / lax.optimization_barrier(jnp.sum(exp_scores, axis=-1, keepdims=True))).astype(jnp.bfloat16)
        return jnp.dot(softmax_out, value_head, preferred_element_type=jnp.float32).astype(jnp.bfloat16)
    heads = lax.map(one_head, jnp.arange(QUERY_HEAD_TOTAL, dtype=jnp.int32))
    attended = jnp.transpose(heads, (1, 0, 2)).reshape(DOCUMENT_TOKENS, QUERY_HEAD_TOTAL * HEAD_SIZE)
    branch = jnp.dot(attended, out_weight, preferred_element_type=jnp.float32).astype(jnp.bfloat16)
    return (floats + branch.astype(jnp.float32)).astype(jnp.bfloat16)

def reference(acts, norm_gain, w_query, section_key_weights, section_value_weights, w_out):
    results = [layer(acts[section], norm_gain[section], w_query[section], section_key_weights[section], section_value_weights[section], w_out[section]) for section in range(RELAY_SECTIONS)]
    stacked = jnp.stack(results)
    return jnp.concatenate([stacked[-1:], stacked[:-1]], axis=0)
```

```python
import functools
import math

import jax
import jax.numpy as jnp
from jax import lax
from jax.experimental import pallas as pl
from jax.experimental.pallas import tpu as pltpu
from jax.sharding import PartitionSpec as P

HEAD = 128
EPS = 1e-05
ROPE_BASE = 500000.0
SEQ = 32
BF = jnp.bfloat16
F32 = jnp.float32
VMEM = pl.BlockSpec(memory_space=pltpu.VMEM)
SMEM = pl.BlockSpec(memory_space=pltpu.SMEM)
Q_FOLD = math.log2(math.e) / math.sqrt(HEAD)


def send(x, move):
    pairs = []
    for s in range(4):
        for d in range(SEQ):
            xh, core, xl, y, z = move(s // 2, s % 2, d // 16, d // 4 % 4, d % 4)
            pairs.append((s * SEQ + d, (xh * 2 + core) * SEQ + xl * 16 + y % 4 * 4 + z % 4))
    return lax.ppermute(x, ("section", "seq"), pairs)


def along_y(x, k):
    return send(x, lambda xh, c, b, y, z: (xh, c, b, y + k, z))


def along_z(x, k):
    return send(x, lambda xh, c, b, y, z: (xh, c, b, y, z + k))


def swap_core(x):
    return send(x, lambda xh, c, b, y, z: (xh, 1 - c, b, y, z))


def params(**kw):
    return pltpu.CompilerParams(vmem_limit_bytes=60 * 1024 * 1024, **kw)


def cost(flops, nbytes, transcendentals=0):
    return pl.CostEstimate(flops=flops, bytes_accessed=nbytes, transcendentals=transcendentals)


def query_kernel(place, x_ref, w_ref, c_ref, s_ref, o_ref):
    u = jnp.dot(x_ref[...], w_ref[0], preferred_element_type=F32)
    for h in range(4):
        v = u[:, h * HEAD : (h + 1) * HEAD]
        o_ref[0, :, h * HEAD : (h + 1) * HEAD] = (
            (v * c_ref[...] + pltpu.roll(v, 64, 1) * s_ref[...]) * Q_FOLD
        ).astype(BF)


def queries(place, x, w, c, s):
    return pl.pallas_call(
        query_kernel,
        grid_spec=pltpu.PrefetchScalarGridSpec(
            num_scalar_prefetch=1,
            grid=(4,),
            in_specs=[
                pl.BlockSpec((256, 4096), lambda k, p: (0, 0)),
                pl.BlockSpec((1, 4096, 512), lambda k, p: (0, 0, lax.rem(p[3] + k, 4))),
                pl.BlockSpec((256, HEAD), lambda k, p: (0, 0)),
                pl.BlockSpec((256, HEAD), lambda k, p: (0, 0)),
            ],
            out_specs=pl.BlockSpec((1, 256, 512), lambda k, p: (k, 0, 0)),
        ),
        out_shape=jax.ShapeDtypeStruct((4, 256, 512), BF),
        compiler_params=params(),
        cost_estimate=cost(2 * 256 * 4096 * 2048, 20 << 20),
        name="queries",
    )(place, x, w, c, s)


def kv_kernel(place, own, oth, c_ref, s_ref, *rest):
    first, second = rest[0:4], rest[4:8]
    o_ref, acc = rest[8:]
    core, y, z = place[0], place[2], place[3]

    def columns(ref, blocks):
        return jnp.concatenate(
            [ref[:, pl.ds(pl.multiple_of(b * 128, 128), 128)] for b in blocks], axis=1
        )

    for which in range(8):
        if which < 4:
            w = first[which]
            blocks = [core * 16 + lax.rem(y + 4 - m, 4) * 4 + lax.rem(z + 4 - which, 4) for m in range(4)]
        else:
            w = second[which - 4]
            blocks = [
                (1 - core) * 16 + lax.rem(y + 8 - which, 4) * 4 + lax.rem(z + 4 - j, 4)
                for j in range(4)
            ]
        for t, ref in enumerate((own, oth)):
            part = jnp.dot(columns(ref, blocks), w[...], preferred_element_type=F32)
            if which == 0:
                acc[t] = part
            else:
                acc[t] += part
    for t in range(2):
        row = pl.multiple_of(lax.select(t == 0, core, 1 - core) * 256, 256)
        for k in range(4):
            v = acc[t, :, pl.ds(pl.multiple_of(lax.rem(z + k, 4) * HEAD, HEAD), HEAD)]
            o_ref[k, pl.ds(row, 256), :] = (v * c_ref[t] + pltpu.roll(v, 64, 1) * s_ref[t]).astype(BF)


def keys_or_values(place, own, oth, c, s, first, second):
    return pl.pallas_call(
        kv_kernel,
        in_specs=[SMEM] + [VMEM] * 12,
        out_specs=VMEM,
        out_shape=jax.ShapeDtypeStruct((4, 512, HEAD), BF),
        scratch_shapes=[pltpu.VMEM((2, 256, 512), F32)],
        compiler_params=params(),
        cost_estimate=cost(2 * 512 * 4096 * 512, 9 << 20),
        name="keys_or_values",
    )(place, own, oth, c, s, *first, *second)


def attend_kernel(place, *refs):
    q = refs[0:4]
    mine, other = refs[4:8], refs[8:12]
    o_ref, kv, vv = refs[12:]
    core = place[0]
    vv[:, :, HEAD:] = jnp.ones((4, 2048, HEAD), BF)
    for m in range(4):
        kv[m, core] = mine[m][...]
        kv[m, 1 - core] = other[m][...]
        vv[m, :, :HEAD] = kv[m, 1]

    for k in range(4):
        for h in range(4):
            qb = q[k][:, h * HEAD : (h + 1) * HEAD]

            def step(m, carry):
                top, acc = carry
                sc = lax.dot_general(qb, kv[m, 0], (((1,), (1,)), ((), ())), preferred_element_type=F32)
                new = jnp.maximum(top, jnp.max(sc, axis=1, keepdims=True))
                p = jnp.exp2(sc - new).astype(BF)
                acc = acc * jnp.exp2(top - new) + jnp.dot(p, vv[m], preferred_element_type=F32)
                return new, acc

            top = jnp.full((256, 1), -1e30, F32)
            _, acc = lax.fori_loop(0, 4, step, (top, jnp.zeros((256, 256), F32)))
            o_ref[k, :, h * HEAD : (h + 1) * HEAD] = (acc[:, :HEAD] / acc[:, HEAD:]).astype(BF)


def attend(place, q, mine, other):
    return pl.pallas_call(
        attend_kernel,
        in_specs=[SMEM] + [VMEM] * 12,
        out_specs=VMEM,
        out_shape=jax.ShapeDtypeStruct((4, 256, 512), BF),
        scratch_shapes=[pltpu.VMEM((4, 2, 2048, HEAD), BF), pltpu.VMEM((4, 2048, 2 * HEAD), BF)],
        compiler_params=params(),
        cost_estimate=cost(4 * 4096 * 8192 * 256, 6 << 20, 4096 * 8192),
        name="attend",
    )(place, *q, *mine, *other)


def project_kernel(place, *refs):
    att, own, oth, o_ref = refs[0:4], refs[4], refs[5], refs[6]
    z = place[3]
    for half, w in enumerate((own, oth)):
        for j in range(4):
            row = pl.multiple_of(lax.rem(z + 4 - j, 4) * 512, 512)
            wj = jnp.concatenate([w[m, pl.ds(row, 512), :] for m in range(4)], axis=1)
            for k in range(4):
                part = jnp.dot(att[j][(k - j) % 4], wj, preferred_element_type=F32)
                acc = refs[7]
                if j == 0:
                    acc[k] = part
                elif j < 3:
                    acc[k] += part
                else:
                    o_ref[k, :, half * 512 : (half + 1) * 512] = (acc[k] + part).astype(BF)


def project(place, att, own, oth):
    return pl.pallas_call(
        project_kernel,
        in_specs=[SMEM] + [VMEM] * 6,
        out_specs=VMEM,
        out_shape=jax.ShapeDtypeStruct((4, 256, 1024), BF),
        scratch_shapes=[pltpu.VMEM((4, 256, 512), F32)],
        compiler_params=params(),
        cost_estimate=cost(2 * 1024 * 2048 * 1024, 10 << 20),
        name="project",
    )(place, *att, own, oth)


def residual_kernel(place, acts, *refs):
    branch, o_ref = refs[0:4], refs[4]
    xl, y, z = place[1], place[2], place[3]
    for k in range(4):
        for half in range(2):
            b = xl if half == 0 else 1 - xl
            for m in range(4):
                block = b * 16 + lax.rem(y + 4 - m, 4) * 4 + lax.rem(z + k, 4)
                at = pl.ds(pl.multiple_of(block * 128, 128), 128)
                i = (half * 4 + m) * 128
                o_ref[:, at] = (acts[:, at].astype(F32) + branch[k][:, i : i + 128].astype(F32)).astype(BF)


def residual(place, acts, branch):
    return pl.pallas_call(
        residual_kernel,
        in_specs=[SMEM] + [VMEM] * 5,
        out_specs=VMEM,
        out_shape=jax.ShapeDtypeStruct((256, 4096), BF),
        compiler_params=params(),
        cost_estimate=cost(256 * 4096, 6 << 20),
        name="residual",
    )(place, acts, *branch)


def tables(seq_index):
    freqs = ROPE_BASE ** (-2.0 * jnp.arange(HEAD // 2, dtype=F32) / HEAD)
    positions = seq_index * 256 + jnp.arange(256, dtype=jnp.int32)
    angles = positions.astype(F32)[:, None] * freqs[None, :]
    cosine, sine = jnp.cos(angles), jnp.sin(angles)
    return jnp.concatenate([cosine, cosine], 1), jnp.concatenate([-sine, sine], 1)


def turn(xh, c, b, y, z):
    return xh, b, c, y, z


def body(acts, norm_gain, w_query, w_key, w_value, w_out):
    section, seq = lax.axis_index("section"), lax.axis_index("seq")
    core, xl, y, z = section % 2, seq // 16, seq // 4 % 4, seq % 4
    place = jnp.stack([core, xl, y, z]).astype(jnp.int32)
    tokens = acts[0]
    low = xl == 0
    half0 = send(jnp.where(low, w_key[0], w_value[0]), turn)
    half1 = send(
        jnp.where(low, w_value[0], w_key[0]), lambda xh, c, b, y, z: (xh, 1 - b, c, y, z)
    )
    floats = tokens.astype(F32)
    normed = (
        floats * lax.rsqrt(jnp.mean(floats * floats, axis=-1, keepdims=True) + EPS) * norm_gain[0]
    ).astype(BF)
    own = send(normed, turn)
    other = swap_core(own)
    first = jnp.concatenate([half0] + [along_y(half0, m) for m in (1, 2, 3)], 0)
    second = jnp.concatenate([half1] + [along_z(half1, j) for j in (1, 2, 3)], 0)
    firsts = [first] + [along_z(first, j) for j in (1, 2, 3)]
    seconds = [second] + [along_y(second, m) for m in (1, 2, 3)]

    cos_n, sin_n = tables(seq)
    q = queries(place, normed, w_query, cos_n, sin_n)
    q = [
        send(q[k], lambda xh, c, b, y, z, k=k: (xh, b, c, y, z + k)) for k in range(4)
    ]

    is_key = core == 0
    rope = [tables(b * 16 + y * 4 + z) for b in (core, 1 - core)]
    cos_k = jnp.where(is_key, jnp.stack([t[0] for t in rope]), 1.0)
    sin_k = jnp.where(is_key, jnp.stack([t[1] for t in rope]), 0.0)
    kv = keys_or_values(place, own, other, cos_k, sin_k, firsts, seconds)
    kv = jnp.concatenate([kv[0]] + [along_z(kv[k], k) for k in (1, 2, 3)], 0)
    mine = [kv] + [along_y(kv, m) for m in (1, 2, 3)]
    theirs = [swap_core(a) for a in mine]
    att = attend(place, q, mine, theirs)

    w_own = send(w_out[0], turn)
    w_own = jnp.stack([w_own] + [along_y(w_own, m) for m in (1, 2, 3)])
    w_other = swap_core(w_own)
    atts = [att] + [along_z(att, j) for j in (1, 2, 3)]
    branch = project(place, atts, w_own, w_other)

    def home(k):
        def move(xh, c, b, y, z):
            s = (2 * xh + b + 1) % 4
            return s // 2, s % 2, c, y, z - k

        return move

    branch = [send(branch[k], home(k)) for k in range(4)]

    def onward(xh, c, b, y, z):
        s = (2 * xh + c + 1) % 4
        return s // 2, s % 2, b, y, z

    return residual(place, send(tokens, onward), branch)[None]


def solution(mesh):
    return jax.shard_map(
        body,
        mesh=mesh,
        in_specs=(
            P("section", "seq", None),
            P("section", None),
            P("section", None, None),
            P("section", "seq", None),
            P("section", "seq", None),
            P("section", None, "seq"),
        ),
        out_specs=P("section", "seq", None),
        check_vma=False,
    )
```

```python
import functools
import math

import jax
import jax.numpy as jnp
from jax import lax
from jax.experimental import pallas as pl
from jax.experimental.pallas import tpu as pltpu
from jax.sharding import PartitionSpec as P

HEAD = 128
EPS = 1e-05
ROPE_BASE = 500000.0
SEQ = 32
BF = jnp.bfloat16
F32 = jnp.float32
VMEM = pl.BlockSpec(memory_space=pltpu.VMEM)
SMEM = pl.BlockSpec(memory_space=pltpu.SMEM)
ROWS = 512
Q_FOLD = math.log2(math.e) / math.sqrt(HEAD)


def send(x, move):
    pairs = []
    for s in range(4):
        for d in range(SEQ):
            xh, core, xl, y, z = move(s // 2, s % 2, d // 16, d // 4 % 4, d % 4)
            pairs.append((s * SEQ + d, (xh * 2 + core) * SEQ + xl * 16 + y % 4 * 4 + z % 4))
    return lax.ppermute(x, ("section", "seq"), pairs)


def along_y(x, k):
    return send(x, lambda xh, c, b, y, z: (xh, c, b, y + k, z))


def along_z(x, k):
    return send(x, lambda xh, c, b, y, z: (xh, c, b, y, z + k))


def swap_core(x):
    return send(x, lambda xh, c, b, y, z: (xh, 1 - c, b, y, z))


def params(**kw):
    return pltpu.CompilerParams(vmem_limit_bytes=60 * 1024 * 1024, **kw)


def cost(flops, nbytes, transcendentals=0):
    return pl.CostEstimate(flops=flops, bytes_accessed=nbytes, transcendentals=transcendentals)


def query_kernel(place, x_ref, w_ref, c_ref, s_ref, o_ref):
    u = jnp.dot(x_ref[...], w_ref[0], preferred_element_type=F32)
    for h in range(4):
        v = u[:, h * HEAD : (h + 1) * HEAD]
        o_ref[0, :, h * HEAD : (h + 1) * HEAD] = (
            (v * c_ref[...] + pltpu.roll(v, 64, 1) * s_ref[...]) * Q_FOLD
        ).astype(BF)


def queries(place, x, w, c, s):
    return pl.pallas_call(
        query_kernel,
        grid_spec=pltpu.PrefetchScalarGridSpec(
            num_scalar_prefetch=1,
            grid=(4,),
            in_specs=[
                pl.BlockSpec((256, 4096), lambda k, p: (0, 0)),
                pl.BlockSpec((1, 4096, 512), lambda k, p: (0, 0, lax.rem(p[3] + k, 4))),
                pl.BlockSpec((256, HEAD), lambda k, p: (0, 0)),
                pl.BlockSpec((256, HEAD), lambda k, p: (0, 0)),
            ],
            out_specs=pl.BlockSpec((1, 256, 512), lambda k, p: (k, 0, 0)),
        ),
        out_shape=jax.ShapeDtypeStruct((4, 256, 512), BF),
        compiler_params=params(),
        cost_estimate=cost(2 * 256 * 4096 * 2048, 20 << 20),
        name="queries",
    )(place, x, w, c, s)


def kv_kernel(place, own, oth, c_ref, s_ref, *rest):
    first, second = rest[0:4], rest[4:8]
    o_ref, acc = rest[8:]
    core, y, z = place[0], place[2], place[3]

    def columns(ref, blocks):
        return jnp.concatenate(
            [ref[:, pl.ds(pl.multiple_of(b * 128, 128), 128)] for b in blocks], axis=1
        )

    for which in range(8):
        if which < 4:
            w = first[which]
            blocks = [core * 16 + lax.rem(y + 4 - m, 4) * 4 + lax.rem(z + 4 - which, 4) for m in range(4)]
        else:
            w = second[which - 4]
            blocks = [
                (1 - core) * 16 + lax.rem(y + 8 - which, 4) * 4 + lax.rem(z + 4 - j, 4)
                for j in range(4)
            ]
        for t, ref in enumerate((own, oth)):
            part = jnp.dot(columns(ref, blocks), w[...], preferred_element_type=F32)
            if which == 0:
                acc[t] = part
            else:
                acc[t] += part
    for t in range(2):
        row = pl.multiple_of(lax.select(t == 0, core, 1 - core) * 256, 256)
        for k in range(4):
            v = acc[t, :, pl.ds(pl.multiple_of(lax.rem(z + k, 4) * HEAD, HEAD), HEAD)]
            o_ref[k, pl.ds(row, 256), :] = (v * c_ref[t] + pltpu.roll(v, 64, 1) * s_ref[t]).astype(BF)


def keys_or_values(place, own, oth, c, s, first, second):
    return pl.pallas_call(
        kv_kernel,
        in_specs=[SMEM] + [VMEM] * 12,
        out_specs=VMEM,
        out_shape=jax.ShapeDtypeStruct((4, 512, HEAD), BF),
        scratch_shapes=[pltpu.VMEM((2, 256, 512), F32)],
        compiler_params=params(),
        cost_estimate=cost(2 * 512 * 4096 * 512, 9 << 20),
        name="keys_or_values",
    )(place, own, oth, c, s, *first, *second)


def lanes_summed(e):
    total = e[:, :HEAD]
    for i in range(HEAD, e.shape[1], HEAD):
        total = total + e[:, i : i + HEAD]
    return total


def attend_part(qb, keys, values, tile=2048):
    acc = sums = None
    for k_ref, v_ref in zip(keys, values):
        for i in range(0, 2048, tile):
            sc = lax.dot_general(
                qb, k_ref[i : i + tile, :], (((1,), (1,)), ((), ())), preferred_element_type=F32
            )
            e = jnp.exp2(sc)
            part = jnp.dot(e.astype(BF), v_ref[i : i + tile, :], preferred_element_type=F32)
            acc = part if acc is None else acc + part
            sums = lanes_summed(e) if sums is None else sums + lanes_summed(e)
    return acc, sums


def attend_own_kernel(*refs):
    q, k_ref, v_ref, acc_ref, sum_ref = refs[0:4], refs[4], refs[5], refs[6], refs[7]

    def head(h, _):
        at = pl.ds(pl.multiple_of(h * HEAD, HEAD), HEAD)
        for k in range(0, 4, 2):
            qb = jnp.concatenate([q[k][:, at], q[k + 1][:, at]], axis=0)
            to = slice(k * 256, k * 256 + 512)
            acc_ref[h, to], sum_ref[h, to] = attend_part(qb, [k_ref], [v_ref])
        return 0

    lax.fori_loop(0, 4, head, 0)


def attend_own(q, keys, values):
    return pl.pallas_call(
        attend_own_kernel,
        in_specs=[VMEM] * 6,
        out_specs=[VMEM, VMEM],
        out_shape=[jax.ShapeDtypeStruct((4, 1024, HEAD), F32)] * 2,
        compiler_params=params(),
        cost_estimate=cost(4 * 4096 * 2048 * 256, 6 << 20, 4096 * 2048),
        name="attend_own",
    )(*q, keys, values)


def attend_head_kernel(h, *refs):
    q, keys, values = refs[0:4], refs[4:8], refs[8:12]
    acc_ref, sum_ref, o_ref, qs, lowest = refs[12:]
    for k in range(4):
        qs[k * 256 : (k + 1) * 256] = q[k][:, h * HEAD : (h + 1) * HEAD]
    lowest[...] = jnp.ones((8, HEAD), F32)

    def rows_of(i, _):
        at = pl.ds(pl.multiple_of(i * ROWS, ROWS), ROWS)
        acc, sums = attend_part(qs[at], keys[1:], values[1:])
        total = jnp.sum(sums + sum_ref[0, at], axis=1, keepdims=True)
        o_ref[at] = ((acc + acc_ref[0, at]) / total).astype(BF)
        good = (total >= 2.0**-100) & (total <= 2.0**100)
        lowest[...] = jnp.minimum(lowest[...], jnp.min(good.astype(F32)))
        return 0

    lax.fori_loop(0, 1024 // ROWS, rows_of, 0)

    @pl.when(jnp.min(lowest[...]) < 0.5)
    def _():
        for k in range(4):
            rows = q[k][:, h * HEAD : (h + 1) * HEAD]
            top = jnp.full((256, 1), -3e38, F32)
            acc = jnp.zeros((256, HEAD), F32)
            total = jnp.zeros((256, 1), F32)
            for k_ref, v_ref in zip(keys, values):

                def step(i, carry, k_ref=k_ref, v_ref=v_ref, rows=rows):
                    top, total, acc = carry
                    at = pl.ds(pl.multiple_of(i * 512, 512), 512)
                    sc = lax.dot_general(
                        rows, k_ref[at, :], (((1,), (1,)), ((), ())), preferred_element_type=F32
                    )
                    new = jnp.maximum(top, jnp.max(sc, axis=1, keepdims=True))
                    e, old = jnp.exp2(sc - new), jnp.exp2(top - new)
                    acc = acc * old + jnp.dot(
                        e.astype(BF), v_ref[at, :], preferred_element_type=F32
                    )
                    return new, total * old + jnp.sum(e, axis=1, keepdims=True), acc

                top, total, acc = lax.fori_loop(0, 4, step, (top, total, acc))
            o_ref[k * 256 : (k + 1) * 256] = (acc / total).astype(BF)


def attend_head(h, q, keys, values, acc, sums):
    whole = lambda shape: pl.BlockSpec(shape, lambda i: (0,) * len(shape))
    one = pl.BlockSpec((1, 1024, HEAD), lambda i: (h, 0, 0))
    return pl.pallas_call(
        functools.partial(attend_head_kernel, h),
        grid=(1,),
        in_specs=[whole((256, 512))] * 4 + [whole((2048, HEAD))] * 8 + [one, one],
        out_specs=whole((1024, HEAD)),
        out_shape=jax.ShapeDtypeStruct((1024, HEAD), BF),
        scratch_shapes=[pltpu.VMEM((1024, HEAD), BF), pltpu.VMEM((8, HEAD), F32)],
        compiler_params=params(),
        cost_estimate=cost(4 * 1024 * 6144 * 256, 6 << 20, 1024 * 6144),
        name=f"attend_head{h}",
    )(*q, *keys, *values, acc, sums)


def project_kernel(first, n, place, *refs):
    att = [refs[4 * i : 4 * i + 4] for i in range(n)]
    own, oth = refs[4 * n : 4 * n + 2]
    before = None if first == 0 else refs[4 * n + 2]
    o_ref = refs[-1]
    z = place[3]
    for half, w in enumerate((own, oth)):
        cols = slice(half * 512, (half + 1) * 512)
        rhs = []
        for j in range(4):
            row = pl.multiple_of(lax.rem(z + 4 - j, 4) * 512 + first * HEAD, HEAD)
            rhs.append(
                jnp.concatenate([w[m, pl.ds(row, n * HEAD), :] for m in range(4)], axis=1)
            )
        rhs = jnp.concatenate(rhs, axis=0)
        for k in range(4):
            rows = [slice((k - j) % 4 * 256, (k - j) % 4 * 256 + 256) for j in range(4)]
            lhs = jnp.concatenate(
                [att[i][j][rows[j]] for j in range(4) for i in range(n)], axis=1
            )
            total = jnp.dot(lhs, rhs, preferred_element_type=F32)
            if before is not None:
                total = total + before[k, :, cols]
            o_ref[k, :, cols] = total.astype(o_ref.dtype)


def project(first, place, att, own, oth, before=None):
    last, n = before is not None, len(att)
    return pl.pallas_call(
        functools.partial(project_kernel, first, n),
        in_specs=[SMEM] + [VMEM] * (4 * n + 2 + last),
        out_specs=VMEM,
        out_shape=jax.ShapeDtypeStruct((4, 256, 1024), BF if last else F32),
        compiler_params=params(),
        cost_estimate=cost(1024 * 1024 * n * 1024, 10 << 20),
        name=f"project{first}",
    )(place, *[a for head in att for a in head], own, oth, *([before] if last else []))


def residual_kernel(place, acts, *refs):
    branch, o_ref = refs[0:4], refs[4]
    xl, y, z = place[1], place[2], place[3]
    for k in range(4):
        for half in range(2):
            b = xl if half == 0 else 1 - xl
            for m in range(4):
                block = b * 16 + lax.rem(y + 4 - m, 4) * 4 + lax.rem(z + k, 4)
                at = pl.ds(pl.multiple_of(block * 128, 128), 128)
                i = (half * 4 + m) * 128
                o_ref[:, at] = (acts[:, at].astype(F32) + branch[k][:, i : i + 128].astype(F32)).astype(BF)


def residual(place, acts, branch):
    return pl.pallas_call(
        residual_kernel,
        in_specs=[SMEM] + [VMEM] * 5,
        out_specs=VMEM,
        out_shape=jax.ShapeDtypeStruct((256, 4096), BF),
        compiler_params=params(),
        cost_estimate=cost(256 * 4096, 6 << 20),
        name="residual",
    )(place, acts, *branch)


def tables(seq_index):
    freqs = ROPE_BASE ** (-2.0 * jnp.arange(HEAD // 2, dtype=F32) / HEAD)
    positions = seq_index * 256 + jnp.arange(256, dtype=jnp.int32)
    angles = positions.astype(F32)[:, None] * freqs[None, :]
    cosine, sine = jnp.cos(angles), jnp.sin(angles)
    return jnp.concatenate([cosine, cosine], 1), jnp.concatenate([-sine, sine], 1)


def turn(xh, c, b, y, z):
    return xh, b, c, y, z


def after(x, *ready):
    return lax.optimization_barrier((x, *ready))[0]


def body(acts, norm_gain, w_query, w_key, w_value, w_out):
    section, seq = lax.axis_index("section"), lax.axis_index("seq")
    core, xl, y, z = section % 2, seq // 16, seq // 4 % 4, seq % 4
    place = jnp.stack([core, xl, y, z]).astype(jnp.int32)
    tokens = acts[0]
    low = xl == 0
    half0 = send(jnp.where(low, w_key[0], w_value[0]), turn)
    half1 = send(
        jnp.where(low, w_value[0], w_key[0]), lambda xh, c, b, y, z: (xh, 1 - b, c, y, z)
    )
    floats = tokens.astype(F32)
    normed = (
        floats * lax.rsqrt(jnp.mean(floats * floats, axis=-1, keepdims=True) + EPS) * norm_gain[0]
    ).astype(BF)
    own = send(after(normed, half0, half1), turn)
    first = jnp.concatenate([half0] + [along_y(half0, m) for m in (1, 2, 3)], 0)
    second = jnp.concatenate([half1] + [along_z(half1, j) for j in (1, 2, 3)], 0)

    cos_n, sin_n = tables(seq)
    q = queries(place, after(normed, first, second), w_query, cos_n, sin_n)
    firsts = {j: along_z(first, j) for j in (1, 3)}
    seconds = {m: along_y(second, m) for m in (1, 3)}
    near = firsts[1], firsts[3], seconds[1], seconds[3]
    firsts[2], seconds[2] = along_z(first, 2), along_y(second, 2)
    firsts = [first] + [firsts[j] for j in (1, 2, 3)]
    seconds = [second] + [seconds[m] for m in (1, 2, 3)]
    other = swap_core(after(own, *near))
    q = after(q, *firsts, *seconds)
    q = [
        send(q[k], lambda xh, c, b, y, z, k=k: (xh, b, c, y, z + k)) for k in range(4)
    ]

    is_key = core == 0
    rope = [tables(b * 16 + y * 4 + z) for b in (core, 1 - core)]
    cos_k = jnp.where(is_key, jnp.stack([t[0] for t in rope]), 1.0)
    sin_k = jnp.where(is_key, jnp.stack([t[1] for t in rope]), 0.0)
    kv = keys_or_values(place, own, other, cos_k, sin_k, firsts, seconds)
    kv = jnp.concatenate([kv[0]] + [along_z(after(kv[k], *q), k) for k in (1, 2, 3)], 0)
    mine = [kv] + [along_y(kv, m) for m in (1, 2, 3)]
    theirs = [swap_core(kv)]
    def in_order(a, b):
        return jnp.where(is_key, a, b), jnp.where(is_key, b, a)

    pairs = [in_order(mine[0], theirs[0])]
    acc, sums = attend_own(q, *pairs[0])
    theirs += [swap_core(after(mine[m], acc)) for m in (1, 2, 3)]
    pairs += [in_order(mine[m], theirs[m]) for m in (1, 2, 3)]
    keys, values = zip(*pairs)
    w_own = send(after(w_out[0], kv), turn)
    passed = send(after(tokens, *theirs), onward)
    w_send = after(w_own, *theirs)
    w_all = [w_own, along_y(w_send, 1), None, along_y(w_send, 3)]
    heads = []
    for h in range(4):
        att = attend_head(h, q, keys, values, acc, sums)
        out = after(att, *heads[-1][1:]) if heads else att
        heads.append([att] + [along_z(out, j) for j in (1, 2, 3)])
        if h == 0:
            w_all[2] = along_y(after(w_own, w_all[1], w_all[3], att), 2)
        if h == 1:
            w_own = jnp.stack([after(w, att, *heads[0][1:]) for w in w_all])
            w_other = swap_core(w_own)
        ready = [att] + (heads[h - 1][1:] if h else [])
        acc, sums = after(acc, *ready), after(sums, *ready)
    heads[0][0] = after(heads[0][0], att)
    branch = project(0, place, heads[:3], w_own, w_other)
    branch = project(3, place, heads[3:], w_own, w_other, branch)

    def home(k):
        def move(xh, c, b, y, z):
            s = (2 * xh + b + 1) % 4
            return s // 2, s % 2, c, y, z - k

        return move

    branch = [send(branch[k], home(k)) for k in range(4)]
    return residual(place, passed, branch)[None]


def onward(xh, c, b, y, z):
    s = (2 * xh + c + 1) % 4
    return s // 2, s % 2, b, y, z


def solution(mesh):
    return jax.shard_map(
        body,
        mesh=mesh,
        in_specs=(
            P("section", "seq", None),
            P("section", None),
            P("section", None, None),
            P("section", "seq", None),
            P("section", "seq", None),
            P("section", None, "seq"),
        ),
        out_specs=P("section", "seq", None),
        check_vma=False,
    )
```

```python
import functools
import math

import jax
import jax.numpy as jnp
from jax import lax
from jax.experimental import pallas as pl
from jax.experimental.pallas import tpu as pltpu
from jax.sharding import PartitionSpec as P

HEAD = 128
EPS = 1e-05
ROPE_BASE = 500000.0
SEQ = 32
BF = jnp.bfloat16
F32 = jnp.float32
VMEM = pl.BlockSpec(memory_space=pltpu.VMEM)
SMEM = pl.BlockSpec(memory_space=pltpu.SMEM)
ROWS = 512
Q_FOLD = math.log2(math.e) / math.sqrt(HEAD)


def send(x, move):
    pairs = []
    for s in range(4):
        for d in range(SEQ):
            xh, core, xl, y, z = move(s // 2, s % 2, d // 16, d // 4 % 4, d % 4)
            pairs.append((s * SEQ + d, (xh * 2 + core) * SEQ + xl * 16 + y % 4 * 4 + z % 4))
    return lax.ppermute(x, ("section", "seq"), pairs)


def along_y(x, k):
    return send(x, lambda xh, c, b, y, z: (xh, c, b, y + k, z))


def along_z(x, k):
    return send(x, lambda xh, c, b, y, z: (xh, c, b, y, z + k))


def swap_core(x):
    return send(x, lambda xh, c, b, y, z: (xh, 1 - c, b, y, z))


def params(**kw):
    return pltpu.CompilerParams(vmem_limit_bytes=36 * 1024 * 1024, **kw)


def cost(flops, nbytes, transcendentals=0):
    return pl.CostEstimate(flops=flops, bytes_accessed=nbytes, transcendentals=transcendentals)


def query_kernel(place, x_ref, w_ref, c_ref, s_ref, *outs):
    u = jnp.dot(x_ref[...], w_ref[0], preferred_element_type=F32)
    done = []
    for h in range(4):
        v = u[:, h * HEAD : (h + 1) * HEAD]
        done.append(((v * c_ref[...] + pltpu.roll(v, 64, 1) * s_ref[...]) * Q_FOLD).astype(BF))
    done = jnp.concatenate(done, axis=1)
    for k in range(4):

        @pl.when(pl.program_id(0) == k)
        def _(k=k):
            outs[k][...] = done


def queries(place, x, w, c, s):
    return pl.pallas_call(
        query_kernel,
        grid_spec=pltpu.PrefetchScalarGridSpec(
            num_scalar_prefetch=1,
            grid=(4,),
            in_specs=[
                pl.BlockSpec((256, 4096), lambda k, p: (0, 0)),
                pl.BlockSpec((1, 4096, 512), lambda k, p: (0, 0, lax.rem(p[3] + k, 4))),
                pl.BlockSpec((256, HEAD), lambda k, p: (0, 0)),
                pl.BlockSpec((256, HEAD), lambda k, p: (0, 0)),
            ],
            out_specs=[pl.BlockSpec((256, 512), lambda k, p: (0, 0))] * 4,
        ),
        out_shape=[jax.ShapeDtypeStruct((256, 512), BF)] * 4,
        compiler_params=params(),
        cost_estimate=cost(2 * 256 * 4096 * 2048, 20 << 20),
        name="queries",
    )(place, x, w, c, s)


def kv_kernel(place, own, oth, c_ref, s_ref, *rest):
    first, second = rest[0:4], rest[4:8]
    outs, acc = rest[8:12], rest[12]
    core, y, z = place[0], place[2], place[3]

    def columns(ref, blocks):
        return jnp.concatenate(
            [ref[:, pl.ds(pl.multiple_of(b * 128, 128), 128)] for b in blocks], axis=1
        )

    for which in range(8):
        if which < 4:
            w = first[which]
            blocks = [core * 16 + lax.rem(y + 4 - m, 4) * 4 + lax.rem(z + 4 - which, 4) for m in range(4)]
        else:
            w = second[which - 4]
            blocks = [
                (1 - core) * 16 + lax.rem(y + 8 - which, 4) * 4 + lax.rem(z + 4 - j, 4)
                for j in range(4)
            ]
        x = jnp.concatenate([columns(own, blocks), columns(oth, blocks)], axis=0)
        part = jnp.dot(x, w[...], preferred_element_type=F32)
        if which == 0:
            acc[...] = part
        else:
            acc[...] += part
    for t in range(2):
        row = pl.multiple_of(lax.select(t == 0, core, 1 - core) * 256, 256)
        for k in range(4):
            v = acc[t * 256 : t * 256 + 256, pl.ds(pl.multiple_of(lax.rem(z + k, 4) * HEAD, HEAD), HEAD)]
            rows = v * c_ref[t] + pltpu.roll(v, 64, 1) * s_ref[t]
            outs[k][pl.ds(row, 256), :] = rows.astype(BF)


def keys_or_values(place, own, oth, c, s, first, second):
    return pl.pallas_call(
        kv_kernel,
        in_specs=[SMEM] + [VMEM] * 12,
        out_specs=[VMEM] * 4,
        out_shape=[jax.ShapeDtypeStruct((512, HEAD), BF)] * 4,
        scratch_shapes=[pltpu.VMEM((512, 512), F32)],
        compiler_params=params(),
        cost_estimate=cost(2 * 512 * 4096 * 512, 9 << 20),
        name="keys_or_values",
    )(place, own, oth, c, s, *first, *second)


def lanes_summed(e):
    total = e[:, :HEAD]
    for i in range(HEAD, e.shape[1], HEAD):
        total = total + e[:, i : i + HEAD]
    return total


def attend_part(qb, keys, values, tile=2048):
    acc = sums = None
    for k_ref, v_ref in zip(keys, values):
        for i in range(0, 2048, tile):
            sc = lax.dot_general(
                qb, k_ref[i : i + tile, :], (((1,), (1,)), ((), ())), preferred_element_type=F32
            )
            e = jnp.exp2(sc)
            part = jnp.dot(e.astype(BF), v_ref[i : i + tile, :], preferred_element_type=F32)
            acc = part if acc is None else acc + part
            sums = lanes_summed(e) if sums is None else sums + lanes_summed(e)
    return acc, sums


def attend_own_kernel(*refs):
    q, k_ref, v_ref, acc_ref, sum_ref = refs[0:4], refs[4], refs[5], refs[6], refs[7]

    def head(h, _):
        at = pl.ds(pl.multiple_of(h * HEAD, HEAD), HEAD)
        for k in range(0, 4, 2):
            qb = jnp.concatenate([q[k][:, at], q[k + 1][:, at]], axis=0)
            to = slice(k * 256, k * 256 + 512)
            acc_ref[h, to], sum_ref[h, to] = attend_part(qb, [k_ref], [v_ref])
        return 0

    lax.fori_loop(0, 4, head, 0)


def attend_own(q, keys, values):
    return pl.pallas_call(
        attend_own_kernel,
        in_specs=[VMEM] * 6,
        out_specs=[VMEM, VMEM],
        out_shape=[jax.ShapeDtypeStruct((4, 1024, HEAD), F32)] * 2,
        compiler_params=params(),
        cost_estimate=cost(4 * 4096 * 2048 * 256, 6 << 20, 4096 * 2048),
        name="attend_own",
    )(*q, keys, values)


def attend_head_kernel(h, *refs):
    q, keys, values = refs[0:4], refs[4:8], refs[8:12]
    acc_ref, sum_ref, o_ref, qs, lowest = refs[12:]
    for k in range(4):
        qs[k * 256 : (k + 1) * 256] = q[k][:, h * HEAD : (h + 1) * HEAD]
    lowest[...] = jnp.ones((8, HEAD), F32)

    def rows_of(i, _):
        at = pl.ds(pl.multiple_of(i * ROWS, ROWS), ROWS)
        acc, sums = attend_part(qs[at], keys[1:], values[1:])
        total = jnp.sum(sums + sum_ref[0, at], axis=1, keepdims=True)
        o_ref[at] = ((acc + acc_ref[0, at]) / total).astype(BF)
        good = (total >= 2.0**-100) & (total <= 2.0**100)
        lowest[...] = jnp.minimum(lowest[...], jnp.min(good.astype(F32)))
        return 0

    lax.fori_loop(0, 1024 // ROWS, rows_of, 0)

    @pl.when(jnp.min(lowest[...]) < 0.5)
    def _():
        for k in range(4):
            rows = q[k][:, h * HEAD : (h + 1) * HEAD]
            top = jnp.full((256, 1), -3e38, F32)
            acc = jnp.zeros((256, HEAD), F32)
            total = jnp.zeros((256, 1), F32)
            for k_ref, v_ref in zip(keys, values):

                def step(i, carry, k_ref=k_ref, v_ref=v_ref, rows=rows):
                    top, total, acc = carry
                    at = pl.ds(pl.multiple_of(i * 512, 512), 512)
                    sc = lax.dot_general(
                        rows, k_ref[at, :], (((1,), (1,)), ((), ())), preferred_element_type=F32
                    )
                    new = jnp.maximum(top, jnp.max(sc, axis=1, keepdims=True))
                    e, old = jnp.exp2(sc - new), jnp.exp2(top - new)
                    acc = acc * old + jnp.dot(
                        e.astype(BF), v_ref[at, :], preferred_element_type=F32
                    )
                    return new, total * old + jnp.sum(e, axis=1, keepdims=True), acc

                top, total, acc = lax.fori_loop(0, 4, step, (top, total, acc))
            o_ref[k * 256 : (k + 1) * 256] = (acc / total).astype(BF)


def attend_head(h, q, keys, values, acc, sums):
    whole = lambda shape: pl.BlockSpec(shape, lambda i: (0,) * len(shape))
    one = pl.BlockSpec((1, 1024, HEAD), lambda i: (h, 0, 0))
    return pl.pallas_call(
        functools.partial(attend_head_kernel, h),
        grid=(1,),
        in_specs=[whole((256, 512))] * 4 + [whole((2048, HEAD))] * 8 + [one, one],
        out_specs=whole((1024, HEAD)),
        out_shape=jax.ShapeDtypeStruct((1024, HEAD), BF),
        scratch_shapes=[pltpu.VMEM((1024, HEAD), BF), pltpu.VMEM((8, HEAD), F32)],
        compiler_params=params(),
        cost_estimate=cost(4 * 1024 * 6144 * 256, 6 << 20, 1024 * 6144),
        name=f"attend_head{h}",
    )(*q, *keys, *values, acc, sums)


def project_kernel(first, n, place, *refs):
    att = [refs[4 * i : 4 * i + 4] for i in range(n)]
    own, oth = refs[4 * n : 4 * n + 2]
    before = None if first == 0 else refs[4 * n + 2]
    outs = refs[4 * n + 2 + (first > 0) :]
    z = place[3]
    for half, w in enumerate((own, oth)):
        cols = slice(half * 512, (half + 1) * 512)
        rhs = []
        for j in range(4):
            row = pl.multiple_of(lax.rem(z + 4 - j, 4) * 512 + first * HEAD, HEAD)
            rhs.append(
                jnp.concatenate([w[m, pl.ds(row, n * HEAD), :] for m in range(4)], axis=1)
            )
        rhs = jnp.concatenate(rhs, axis=0)
        lhs = []
        for k in range(4):
            rows = [slice((k - j) % 4 * 256, (k - j) % 4 * 256 + 256) for j in range(4)]
            lhs.append(
                jnp.concatenate([att[i][j][rows[j]] for j in range(4) for i in range(n)], axis=1)
            )
        total = jnp.dot(jnp.concatenate(lhs, axis=0), rhs, preferred_element_type=F32)
        if before is None:
            outs[0][:, cols] = total
        else:
            total = total + before[:, cols]
            for k in range(4):
                outs[k][:, cols] = total[k * 256 : k * 256 + 256].astype(BF)


def project(first, place, att, own, oth, before=None):
    last, n = before is not None, len(att)
    return pl.pallas_call(
        functools.partial(project_kernel, first, n),
        in_specs=[SMEM] + [VMEM] * (4 * n + 2 + last),
        out_specs=[VMEM] * (4 if last else 1),
        out_shape=[jax.ShapeDtypeStruct((256, 1024), BF)] * 4
        if last
        else [jax.ShapeDtypeStruct((1024, 1024), F32)],
        compiler_params=params(),
        cost_estimate=cost(1024 * 1024 * n * 1024, 10 << 20),
        name=f"project{first}",
    )(place, *[a for head in att for a in head], own, oth, *([before] if last else []))


def residual_kernel(place, acts, *refs):
    branch, o_ref = refs[0:4], refs[4]
    xl, y, z = place[1], place[2], place[3]
    for k in range(4):
        for half in range(2):
            b = xl if half == 0 else 1 - xl
            for m in range(4):
                block = b * 16 + lax.rem(y + 4 - m, 4) * 4 + lax.rem(z + k, 4)
                at = pl.ds(pl.multiple_of(block * 128, 128), 128)
                i = (half * 4 + m) * 128
                o_ref[:, at] = (acts[:, at].astype(F32) + branch[k][:, i : i + 128].astype(F32)).astype(BF)


def residual(place, acts, branch):
    return pl.pallas_call(
        residual_kernel,
        grid=(4,),
        in_specs=[SMEM, pl.BlockSpec((64, 4096), lambda i: (i, 0))]
        + [pl.BlockSpec((64, 1024), lambda i: (i, 0))] * 4,
        out_specs=pl.BlockSpec((64, 4096), lambda i: (i, 0)),
        out_shape=jax.ShapeDtypeStruct((256, 4096), BF),
        compiler_params=params(),
        cost_estimate=cost(256 * 4096, 6 << 20),
        name="residual",
    )(place, acts, *branch)


def tables(seq_index):
    freqs = ROPE_BASE ** (-2.0 * jnp.arange(HEAD // 2, dtype=F32) / HEAD)
    positions = seq_index * 256 + jnp.arange(256, dtype=jnp.int32)
    angles = positions.astype(F32)[:, None] * freqs[None, :]
    cosine, sine = jnp.cos(angles), jnp.sin(angles)
    return jnp.concatenate([cosine, cosine], 1), jnp.concatenate([-sine, sine], 1)


def turn(xh, c, b, y, z):
    return xh, b, c, y, z


def after(x, *ready):
    return lax.optimization_barrier((x, *ready))[0]


def body(acts, norm_gain, w_query, w_key, w_value, w_out):
    section, seq = lax.axis_index("section"), lax.axis_index("seq")
    core, xl, y, z = section % 2, seq // 16, seq // 4 % 4, seq % 4
    place = jnp.stack([core, xl, y, z]).astype(jnp.int32)
    tokens = acts[0]
    low = xl == 0
    mine, cross = jnp.where(low, w_key[0], w_value[0]), jnp.where(low, w_value[0], w_key[0])
    first = [send(mine, lambda xh, c, b, y, z, m=m: (xh, b, c, y + m, z)) for m in range(4)]
    second = [send(cross, lambda xh, c, b, y, z, j=j: (xh, 1 - b, c, y, z + j)) for j in range(4)]
    floats = tokens.astype(F32)
    normed = (
        floats * lax.rsqrt(jnp.mean(floats * floats, axis=-1, keepdims=True) + EPS) * norm_gain[0]
    ).astype(BF)
    own = send(after(normed, *first, *second), turn)
    first, second = jnp.concatenate(first, 0), jnp.concatenate(second, 0)

    cos_n, sin_n = tables(seq)
    q = queries(place, after(normed, first, second), w_query, cos_n, sin_n)
    firsts = {j: along_z(first, j) for j in (1, 3)}
    seconds = {m: along_y(second, m) for m in (1, 3)}
    near = firsts[1], firsts[3], seconds[1], seconds[3]
    firsts[2], seconds[2] = along_z(after(first, *q), 2), along_y(after(second, *q), 2)
    firsts = [first] + [firsts[j] for j in (1, 2, 3)]
    seconds = [second] + [seconds[m] for m in (1, 2, 3)]
    other = swap_core(after(own, *near, *q))
    q = [
        send(after(q[k], firsts[2], seconds[2]), lambda xh, c, b, y, z, k=k: (xh, b, c, y, z + k)) for k in range(4)
    ]

    is_key = core == 0
    rope = [tables(b * 16 + y * 4 + z) for b in (core, 1 - core)]
    cos_k = jnp.where(is_key, jnp.stack([t[0] for t in rope]), 1.0)
    sin_k = jnp.where(is_key, jnp.stack([t[1] for t in rope]), 0.0)
    kv = keys_or_values(place, own, other, cos_k, sin_k, firsts, seconds)
    kv = jnp.concatenate([kv[0]] + [along_z(kv[k], k) for k in (1, 2, 3)], 0)
    mine = [kv] + [along_y(kv, m) for m in (1, 2, 3)]
    theirs = [swap_core(kv)]
    def in_order(a, b):
        return jnp.where(is_key, a, b), jnp.where(is_key, b, a)

    pairs = [in_order(mine[0], theirs[0])]
    acc, sums = attend_own(q, *pairs[0])
    theirs += [swap_core(after(mine[m], acc)) for m in (1, 2, 3)]
    pairs += [in_order(mine[m], theirs[m]) for m in (1, 2, 3)]
    keys, values = zip(*pairs)
    w_own = send(after(w_out[0], kv), turn)
    passed = send(after(tokens, *theirs), onward)
    w_send = after(w_own, *theirs)
    w_all = [w_own, along_y(w_send, 1), None, along_y(w_send, 3)]
    heads = []
    for h in range(4):
        att = attend_head(h, q, keys, values, acc, sums)
        out = after(att, *heads[-1][1:]) if heads else att
        heads.append([att] + [along_z(out, j) for j in (1, 2, 3)])
        if h == 0:
            w_all[2] = along_y(after(w_own, w_all[1], w_all[3], att), 2)
        if h == 1:
            w_own = jnp.stack([after(w, att, *heads[0][1:]) for w in w_all])
            w_other = swap_core(w_own)
        ready = [att] + (heads[h - 1][1:] if h else [])
        acc, sums = after(acc, *ready), after(sums, *ready)
    heads[0][0] = after(heads[0][0], att)
    branch = project(0, place, heads[:3], w_own, w_other)[0]
    branch = project(3, place, heads[3:], w_own, w_other, branch)

    def home(k):
        def move(xh, c, b, y, z):
            s = (2 * xh + b + 1) % 4
            return s // 2, s % 2, c, y, z - k

        return move

    branch = [send(branch[k], home(k)) for k in range(4)]
    return residual(place, passed, branch)[None]


def onward(xh, c, b, y, z):
    s = (2 * xh + c + 1) % 4
    return s // 2, s % 2, b, y, z


def solution(mesh):
    return jax.shard_map(
        body,
        mesh=mesh,
        in_specs=(
            P("section", "seq", None),
            P("section", None),
            P("section", None, None),
            P("section", "seq", None),
            P("section", "seq", None),
            P("section", None, "seq"),
        ),
        out_specs=P("section", "seq", None),
        check_vma=False,
    )
```

```python
import functools
import math

import jax
import jax.numpy as jnp
from jax import lax
from jax.experimental import pallas as pl
from jax.experimental.pallas import tpu as pltpu
from jax.sharding import PartitionSpec as P

HEAD = 128
EPS = 1e-05
ROPE_BASE = 500000.0
SEQ = 32
BF = jnp.bfloat16
F32 = jnp.float32
VMEM = pl.BlockSpec(memory_space=pltpu.VMEM)
SMEM = pl.BlockSpec(memory_space=pltpu.SMEM)
ROWS = 512
GROUPS = ((0, 1), (1, 1), (2, 2))
Q_FOLD = math.log2(math.e) / math.sqrt(HEAD)


def send(x, move):
    pairs = []
    for s in range(4):
        for d in range(SEQ):
            xh, core, xl, y, z = move(s // 2, s % 2, d // 16, d // 4 % 4, d % 4)
            pairs.append((s * SEQ + d, (xh * 2 + core) * SEQ + xl * 16 + y % 4 * 4 + z % 4))
    return lax.ppermute(x, ("section", "seq"), pairs)


def along_y(x, k):
    return send(x, lambda xh, c, b, y, z: (xh, c, b, y + k, z))


def along_z(x, k):
    return send(x, lambda xh, c, b, y, z: (xh, c, b, y, z + k))


def swap_core(x):
    return send(x, lambda xh, c, b, y, z: (xh, 1 - c, b, y, z))


def params(**kw):
    return pltpu.CompilerParams(vmem_limit_bytes=36 * 1024 * 1024, **kw)


def cost(flops, nbytes, transcendentals=0):
    return pl.CostEstimate(flops=flops, bytes_accessed=nbytes, transcendentals=transcendentals)


def query_kernel(place, x_ref, w_ref, c_ref, s_ref, *outs):
    u = jnp.dot(x_ref[...], w_ref[0], preferred_element_type=F32)
    done = []
    for h in range(4):
        v = u[:, h * HEAD : (h + 1) * HEAD]
        done.append(((v * c_ref[...] + pltpu.roll(v, 64, 1) * s_ref[...]) * Q_FOLD).astype(BF))
    done = jnp.concatenate(done, axis=1)
    for k in range(4):

        @pl.when(pl.program_id(0) == k)
        def _(k=k):
            outs[k][...] = done


def queries(place, x, w, c, s):
    return pl.pallas_call(
        query_kernel,
        grid_spec=pltpu.PrefetchScalarGridSpec(
            num_scalar_prefetch=1,
            grid=(4,),
            in_specs=[
                pl.BlockSpec((256, 4096), lambda k, p: (0, 0)),
                pl.BlockSpec((1, 4096, 512), lambda k, p: (0, 0, lax.rem(p[3] + k, 4))),
                pl.BlockSpec((256, HEAD), lambda k, p: (0, 0)),
                pl.BlockSpec((256, HEAD), lambda k, p: (0, 0)),
            ],
            out_specs=[pl.BlockSpec((256, 512), lambda k, p: (0, 0))] * 4,
        ),
        out_shape=[jax.ShapeDtypeStruct((256, 512), BF)] * 4,
        compiler_params=params(),
        cost_estimate=cost(2 * 256 * 4096 * 2048, 20 << 20),
        name="queries",
    )(place, x, w, c, s)


def kv_kernel(place, own, oth, c_ref, s_ref, *rest):
    first, second = rest[0:4], rest[4:8]
    outs, acc = rest[8:12], rest[12]
    core, y, z = place[0], place[2], place[3]

    def columns(ref, blocks):
        return jnp.concatenate(
            [ref[:, pl.ds(pl.multiple_of(b * 128, 128), 128)] for b in blocks], axis=1
        )

    for which in range(8):
        if which < 4:
            w = first[which]
            blocks = [core * 16 + lax.rem(y + 4 - m, 4) * 4 + lax.rem(z + 4 - which, 4) for m in range(4)]
        else:
            w = second[which - 4]
            blocks = [
                (1 - core) * 16 + lax.rem(y + 8 - which, 4) * 4 + lax.rem(z + 4 - j, 4)
                for j in range(4)
            ]
        x = jnp.concatenate([columns(own, blocks), columns(oth, blocks)], axis=0)
        part = jnp.dot(x, w[...], preferred_element_type=F32)
        if which == 0:
            acc[...] = part
        else:
            acc[...] += part
    for t in range(2):
        row = pl.multiple_of(lax.select(t == 0, core, 1 - core) * 256, 256)
        for k in range(4):
            v = acc[t * 256 : t * 256 + 256, pl.ds(pl.multiple_of(lax.rem(z + k, 4) * HEAD, HEAD), HEAD)]
            rows = v * c_ref[t] + pltpu.roll(v, 64, 1) * s_ref[t]
            outs[k][pl.ds(row, 256), :] = rows.astype(BF)


def keys_or_values(place, own, oth, c, s, first, second):
    return pl.pallas_call(
        kv_kernel,
        in_specs=[SMEM] + [VMEM] * 12,
        out_specs=[VMEM] * 4,
        out_shape=[jax.ShapeDtypeStruct((512, HEAD), BF)] * 4,
        scratch_shapes=[pltpu.VMEM((512, 512), F32)],
        compiler_params=params(),
        cost_estimate=cost(2 * 512 * 4096 * 512, 9 << 20),
        name="keys_or_values",
    )(place, own, oth, c, s, *first, *second)


def lanes_summed(e):
    total = e[:, :HEAD]
    for i in range(HEAD, e.shape[1], HEAD):
        total = total + e[:, i : i + HEAD]
    return total


def attend_part(qb, keys, values, tile=2048):
    acc = sums = None
    for k_ref, v_ref in zip(keys, values):
        for i in range(0, 2048, tile):
            sc = lax.dot_general(
                qb, k_ref[i : i + tile, :], (((1,), (1,)), ((), ())), preferred_element_type=F32
            )
            e = jnp.exp2(sc)
            part = jnp.dot(e.astype(BF), v_ref[i : i + tile, :], preferred_element_type=F32)
            acc = part if acc is None else acc + part
            sums = lanes_summed(e) if sums is None else sums + lanes_summed(e)
    return acc, sums


def attend_own_kernel(*refs):
    q, k_ref, v_ref, acc_ref, sum_ref = refs[0:4], refs[4], refs[5], refs[6], refs[7]

    def head(h, _):
        at = pl.ds(pl.multiple_of(h * HEAD, HEAD), HEAD)
        for k in range(0, 4, 2):
            qb = jnp.concatenate([q[k][:, at], q[k + 1][:, at]], axis=0)
            to = pl.ds(pl.multiple_of(h * 1024 + k * 256, 256), 512)
            acc_ref[to], sum_ref[to] = attend_part(qb, [k_ref], [v_ref])
        return 0

    lax.fori_loop(0, 4, head, 0)


def attend_own(q, keys, values):
    return pl.pallas_call(
        attend_own_kernel,
        in_specs=[VMEM] * 6,
        out_specs=[VMEM, VMEM],
        out_shape=[jax.ShapeDtypeStruct((4096, HEAD), F32)] * 2,
        compiler_params=params(),
        cost_estimate=cost(4 * 4096 * 2048 * 256, 6 << 20, 4096 * 2048),
        name="attend_own",
    )(*q, keys, values)


def attend_heads_kernel(h, n, *refs):
    q, keys, values = refs[0:4], refs[4:8], refs[8:12]
    acc_ref, sum_ref, o_ref, qs, lowest = refs[12:]
    for i in range(n):
        for k in range(4):
            to = i * 1024 + k * 256
            qs[to : to + 256] = q[k][:, (h + i) * HEAD : (h + i + 1) * HEAD]
    lowest[...] = jnp.ones((8, HEAD), F32)

    def rows_of(i, _):
        at = pl.ds(pl.multiple_of(i * ROWS, ROWS), ROWS)
        acc, sums = attend_part(qs[at], keys[1:], values[1:])
        total = jnp.sum(sums + sum_ref[at], axis=1, keepdims=True)
        o_ref[at] = ((acc + acc_ref[at]) / total).astype(BF)
        good = (total >= 2.0**-100) & (total <= 2.0**100)
        lowest[...] = jnp.minimum(lowest[...], jnp.min(good.astype(F32)))
        return 0

    lax.fori_loop(0, n * 1024 // ROWS, rows_of, 0)

    @pl.when(jnp.min(lowest[...]) < 0.5)
    def _():
        def again(i, _):
            own = pl.ds(pl.multiple_of(i * 256, 256), 256)
            rows = qs[own]
            top = jnp.full((256, 1), -3e38, F32)
            total, acc = jnp.zeros((256, 1), F32), jnp.zeros((256, HEAD), F32)
            for k_ref, v_ref in zip(keys, values):

                def step(i, carry, k_ref=k_ref, v_ref=v_ref):
                    top, total, acc = carry
                    at = pl.ds(pl.multiple_of(i * 512, 512), 512)
                    sc = lax.dot_general(
                        rows, k_ref[at, :], (((1,), (1,)), ((), ())), preferred_element_type=F32
                    )
                    new = jnp.maximum(top, jnp.max(sc, axis=1, keepdims=True))
                    e, old = jnp.exp2(sc - new), jnp.exp2(top - new)
                    acc = acc * old + jnp.dot(e.astype(BF), v_ref[at, :], preferred_element_type=F32)
                    return new, total * old + jnp.sum(e, axis=1, keepdims=True), acc

                top, total, acc = lax.fori_loop(0, 4, step, (top, total, acc))
            o_ref[own] = (acc / total).astype(BF)
            return 0

        lax.fori_loop(0, n * 4, again, 0)


def attend_heads(h, n, q, keys, values, acc, sums):
    whole = lambda shape: pl.BlockSpec(shape, lambda i: (0,) * len(shape))
    some = pl.BlockSpec((n * 1024, HEAD), lambda i: (h // n, 0))
    return pl.pallas_call(
        functools.partial(attend_heads_kernel, h, n),
        grid=(1,),
        in_specs=[whole((256, 512))] * 4 + [whole((2048, HEAD))] * 8 + [some, some],
        out_specs=whole((n * 1024, HEAD)),
        out_shape=jax.ShapeDtypeStruct((n * 1024, HEAD), BF),
        scratch_shapes=[pltpu.VMEM((n * 1024, HEAD), BF), pltpu.VMEM((8, HEAD), F32)],
        compiler_params=params(),
        cost_estimate=cost(4 * n * 1024 * 6144 * 256, 6 << 20, n * 1024 * 6144),
        name=f"attend_heads{h}",
    )(*q, *keys, *values, acc, sums)


def project_kernel(first, sizes, place, *refs):
    n, count = sum(sizes), 4 * len(sizes)
    att = [(refs[4 * g : 4 * g + 4], i * 1024) for g, size in enumerate(sizes) for i in range(size)]
    own, oth = refs[count : count + 2]
    before = None if first == 0 else refs[count + 2]
    outs = refs[count + 2 + (first > 0) :]
    z = place[3]
    for half, w in enumerate((own, oth)):
        cols = slice(half * 512, (half + 1) * 512)
        rhs = []
        for j in range(4):
            row = pl.multiple_of(lax.rem(z + 4 - j, 4) * 512 + first * HEAD, HEAD)
            rhs.append(
                jnp.concatenate([w[m, pl.ds(row, n * HEAD), :] for m in range(4)], axis=1)
            )
        rhs = jnp.concatenate(rhs, axis=0)
        lhs = []
        for k in range(4):
            rows = [(k - j) % 4 * 256 for j in range(4)]
            lhs.append(
                jnp.concatenate(
                    [
                        ref[j][skip + rows[j] : skip + rows[j] + 256, :]
                        for j in range(4)
                        for ref, skip in att
                    ],
                    axis=1,
                )
            )
        total = jnp.dot(jnp.concatenate(lhs, axis=0), rhs, preferred_element_type=F32)
        if before is None:
            outs[0][:, cols] = total
        else:
            total = total + before[:, cols]
            for k in range(4):
                outs[k][:, cols] = total[k * 256 : k * 256 + 256].astype(BF)


def project(first, place, att, own, oth, before=None):
    last, sizes = before is not None, [group[0].shape[0] // 1024 for group in att]
    n = sum(sizes)
    return pl.pallas_call(
        functools.partial(project_kernel, first, sizes),
        in_specs=[SMEM] + [VMEM] * (4 * len(att) + 2 + last),
        out_specs=[VMEM] * (4 if last else 1),
        out_shape=[jax.ShapeDtypeStruct((256, 1024), BF)] * 4
        if last
        else [jax.ShapeDtypeStruct((1024, 1024), F32)],
        compiler_params=params(),
        cost_estimate=cost(1024 * 1024 * n * 1024, 10 << 20),
        name=f"project{first}",
    )(place, *[a for head in att for a in head], own, oth, *([before] if last else []))


def residual_kernel(place, acts, *refs):
    branch, o_ref = refs[0:4], refs[4]
    xl, y, z = place[1], place[2], place[3]
    for k in range(4):
        for half in range(2):
            b = xl if half == 0 else 1 - xl
            for m in range(4):
                block = b * 16 + lax.rem(y + 4 - m, 4) * 4 + lax.rem(z + k, 4)
                at = pl.ds(pl.multiple_of(block * 128, 128), 128)
                i = (half * 4 + m) * 128
                o_ref[:, at] = (acts[:, at].astype(F32) + branch[k][:, i : i + 128].astype(F32)).astype(BF)


def residual(place, acts, branch):
    return pl.pallas_call(
        residual_kernel,
        grid=(4,),
        in_specs=[SMEM, pl.BlockSpec((64, 4096), lambda i: (i, 0))]
        + [pl.BlockSpec((64, 1024), lambda i: (i, 0))] * 4,
        out_specs=pl.BlockSpec((64, 4096), lambda i: (i, 0)),
        out_shape=jax.ShapeDtypeStruct((256, 4096), BF),
        compiler_params=params(),
        cost_estimate=cost(256 * 4096, 6 << 20),
        name="residual",
    )(place, acts, *branch)


def tables(seq_index):
    freqs = ROPE_BASE ** (-2.0 * jnp.arange(HEAD // 2, dtype=F32) / HEAD)
    positions = seq_index * 256 + jnp.arange(256, dtype=jnp.int32)
    angles = positions.astype(F32)[:, None] * freqs[None, :]
    cosine, sine = jnp.cos(angles), jnp.sin(angles)
    return jnp.concatenate([cosine, cosine], 1), jnp.concatenate([-sine, sine], 1)


def turn(xh, c, b, y, z, flip=0):
    return xh, b ^ flip, c, y, z


def after(x, *ready):
    return lax.optimization_barrier((x, *ready))[0]


def body(acts, norm_gain, w_query, w_key, w_value, w_out):
    section, seq = lax.axis_index("section"), lax.axis_index("seq")
    core, xl, y, z = section % 2, seq // 16, seq // 4 % 4, seq % 4
    place = jnp.stack([core, xl, y, z]).astype(jnp.int32)
    tokens = acts[0]
    low = xl == 0
    mine, cross = jnp.where(low, w_key[0], w_value[0]), jnp.where(low, w_value[0], w_key[0])
    first = [send(mine, lambda xh, c, b, y, z, m=m: turn(xh, c, b, y + m, z)) for m in range(4)]
    second = [send(cross, lambda xh, c, b, y, z, j=j: turn(xh, c, b, y, z + j, 1)) for j in range(4)]
    floats = tokens.astype(F32)
    normed = (
        floats * lax.rsqrt(jnp.mean(floats * floats, axis=-1, keepdims=True) + EPS) * norm_gain[0]
    ).astype(BF)
    own = send(after(normed, *first, *second), turn)
    first, second = jnp.concatenate(first, 0), jnp.concatenate(second, 0)

    cos_n, sin_n = tables(seq)
    q = queries(place, after(normed, first, second), w_query, cos_n, sin_n)
    firsts = {j: along_z(first, j) for j in (1, 3)}
    seconds = {m: along_y(second, m) for m in (1, 3)}
    near = firsts[1], firsts[3], seconds[1], seconds[3]
    firsts[2], seconds[2] = along_z(after(first, *q), 2), along_y(after(second, *q), 2)
    firsts = [first] + [firsts[j] for j in (1, 2, 3)]
    seconds = [second] + [seconds[m] for m in (1, 2, 3)]
    other = swap_core(after(own, *near, *q))
    q = [
        send(after(q[k], firsts[2], seconds[2]), lambda xh, c, b, y, z, k=k: turn(xh, c, b, y, z + k)) for k in range(4)
    ]

    is_key = core == 0
    rope = [tables(b * 16 + y * 4 + z) for b in (core, 1 - core)]
    cos_k = jnp.where(is_key, jnp.stack([t[0] for t in rope]), 1.0)
    sin_k = jnp.where(is_key, jnp.stack([t[1] for t in rope]), 0.0)
    kv = keys_or_values(place, own, other, cos_k, sin_k, firsts, seconds)
    kv = jnp.concatenate([kv[0]] + [along_z(kv[k], k) for k in (1, 2, 3)], 0)
    mine = [kv] + [along_y(kv, m) for m in (1, 2, 3)]
    theirs = [swap_core(kv)]
    def in_order(a, b):
        return jnp.where(is_key, a, b), jnp.where(is_key, b, a)

    pairs = [in_order(mine[0], theirs[0])]
    acc, sums = attend_own(q, *pairs[0])
    theirs += [swap_core(after(mine[m], acc)) for m in (1, 2, 3)]
    pairs += [in_order(mine[m], theirs[m]) for m in (1, 2, 3)]
    keys, values = zip(*pairs)
    w_own = send(after(w_out[0], kv), turn)
    passed = send(after(tokens, theirs[0]), onward)
    w_send = after(w_own, *theirs)
    w_all = [w_own, along_y(w_send, 1), None, along_y(w_send, 3)]
    heads = []
    for h, n in GROUPS:
        att = attend_heads(h, n, q, keys, values, acc, sums)
        out = after(att, *heads[-1][1:]) if heads else att
        heads.append([att] + [along_z(out, j) for j in (1, 2, 3)])
        if len(heads) == 1:
            w_all[2] = along_y(after(w_own, w_all[1], w_all[3], att), 2)
        if len(heads) == 2:
            w_own = jnp.stack([after(w, att, *heads[0][1:]) for w in w_all])
            w_other = swap_core(w_own)
        ready = [att] + (heads[-2][1:] if heads[1:] else [])
        if len(heads) == len(GROUPS) - 1:
            ready.append(passed)
        acc, sums = after(acc, *ready), after(sums, *ready)
    heads[0][0] = after(heads[0][0], att)
    branch = project(0, place, heads[:-1], w_own, w_other)[0]
    branch = project(GROUPS[-1][0], place, heads[-1:], w_own, w_other, branch)

    def home(k):
        def move(xh, c, b, y, z):
            s = (2 * xh + b + 1) % 4
            return s // 2, s % 2, c, y, z - k

        return move

    branch = [send(branch[k], home(k)) for k in range(4)]
    return residual(place, passed, branch)[None]


def onward(xh, c, b, y, z):
    s = (2 * xh + c + 1) % 4
    return s // 2, s % 2, b, y, z


def solution(mesh):
    return jax.shard_map(
        body,
        mesh=mesh,
        in_specs=(
            P("section", "seq", None),
            P("section", None),
            P("section", None, None),
            P("section", "seq", None),
            P("section", "seq", None),
            P("section", None, "seq"),
        ),
        out_specs=P("section", "seq", None),
        check_vma=False,
    )
```

```python
import functools
import math

import jax
import jax.numpy as jnp
from jax import lax
from jax.experimental import pallas as pl
from jax.experimental.pallas import tpu as pltpu
from jax.sharding import PartitionSpec as P

HEAD = 128
EPS = 1e-05
ROPE_BASE = 500000.0
SEQ = 32
BF = jnp.bfloat16
F32 = jnp.float32
VMEM = pl.BlockSpec(memory_space=pltpu.VMEM)
SMEM = pl.BlockSpec(memory_space=pltpu.SMEM)
ROWS = 512
GROUPS = ((0, 2), (2, 2))
Q_FOLD = math.log2(math.e) / math.sqrt(HEAD)


def send(x, move):
    pairs = []
    for s in range(4):
        for d in range(SEQ):
            xh, core, xl, y, z = move(s // 2, s % 2, d // 16, d // 4 % 4, d % 4)
            pairs.append((s * SEQ + d, (xh * 2 + core) * SEQ + xl * 16 + y % 4 * 4 + z % 4))
    return lax.ppermute(x, ("section", "seq"), pairs)


def along_y(x, k):
    return send(x, lambda xh, c, b, y, z: (xh, c, b, y + k, z))


def along_z(x, k):
    return send(x, lambda xh, c, b, y, z: (xh, c, b, y, z + k))


def swap_core(x):
    return send(x, lambda xh, c, b, y, z: (xh, 1 - c, b, y, z))


def params(**kw):
    return pltpu.CompilerParams(vmem_limit_bytes=36 * 1024 * 1024, **kw)


def cost(flops, nbytes, transcendentals=0):
    return pl.CostEstimate(flops=flops, bytes_accessed=nbytes, transcendentals=transcendentals)


def query_kernel(place, x_ref, w_ref, c_ref, s_ref, *outs):
    u = jnp.dot(x_ref[...], w_ref[0], preferred_element_type=F32)
    done = []
    for h in range(4):
        v = u[:, h * HEAD : (h + 1) * HEAD]
        done.append(((v * c_ref[...] + pltpu.roll(v, 64, 1) * s_ref[...]) * Q_FOLD).astype(BF))
    done = jnp.concatenate(done, axis=1)
    for k in range(4):

        @pl.when(pl.program_id(0) == k)
        def _(k=k):
            outs[k][...] = done


def queries(place, x, w, c, s):
    return pl.pallas_call(
        query_kernel,
        grid_spec=pltpu.PrefetchScalarGridSpec(
            num_scalar_prefetch=1,
            grid=(4,),
            in_specs=[
                pl.BlockSpec((256, 4096), lambda k, p: (0, 0)),
                pl.BlockSpec((1, 4096, 512), lambda k, p: (0, 0, lax.rem(p[3] + k, 4))),
                pl.BlockSpec((256, HEAD), lambda k, p: (0, 0)),
                pl.BlockSpec((256, HEAD), lambda k, p: (0, 0)),
            ],
            out_specs=[pl.BlockSpec((256, 512), lambda k, p: (0, 0))] * 4,
        ),
        out_shape=[jax.ShapeDtypeStruct((256, 512), BF)] * 4,
        compiler_params=params(),
        cost_estimate=cost(2 * 256 * 4096 * 2048, 20 << 20),
        name="queries",
    )(place, x, w, c, s)


def kv_kernel(place, own, oth, c_ref, s_ref, *rest):
    first, second = rest[0:4], rest[4:8]
    outs, acc = rest[8:12], rest[12]
    core, y, z = place[0], place[2], place[3]

    def columns(ref, blocks):
        return jnp.concatenate(
            [ref[:, pl.ds(pl.multiple_of(b * 128, 128), 128)] for b in blocks], axis=1
        )

    for which in range(8):
        if which < 4:
            w = first[which]
            blocks = [core * 16 + lax.rem(y + 4 - m, 4) * 4 + lax.rem(z + 4 - which, 4) for m in range(4)]
        else:
            w = second[which - 4]
            blocks = [
                (1 - core) * 16 + lax.rem(y + 8 - which, 4) * 4 + lax.rem(z + 4 - j, 4)
                for j in range(4)
            ]
        x = jnp.concatenate([columns(own, blocks), columns(oth, blocks)], axis=0)
        part = jnp.dot(x, w[...], preferred_element_type=F32)
        if which == 0:
            acc[...] = part
        else:
            acc[...] += part
    for t in range(2):
        row = pl.multiple_of(lax.select(t == 0, core, 1 - core) * 256, 256)
        for k in range(4):
            v = acc[t * 256 : t * 256 + 256, pl.ds(pl.multiple_of(lax.rem(z + k, 4) * HEAD, HEAD), HEAD)]
            rows = v * c_ref[t] + pltpu.roll(v, 64, 1) * s_ref[t]
            outs[k][pl.ds(row, 256), :] = rows.astype(BF)


def keys_or_values(place, own, oth, c, s, first, second):
    return pl.pallas_call(
        kv_kernel,
        in_specs=[SMEM] + [VMEM] * 12,
        out_specs=[VMEM] * 4,
        out_shape=[jax.ShapeDtypeStruct((512, HEAD), BF)] * 4,
        scratch_shapes=[pltpu.VMEM((512, 512), F32)],
        compiler_params=params(),
        cost_estimate=cost(2 * 512 * 4096 * 512, 9 << 20),
        name="keys_or_values",
    )(place, own, oth, c, s, *first, *second)


def lanes_summed(e):
    total = e[:, :HEAD]
    for i in range(HEAD, e.shape[1], HEAD):
        total = total + e[:, i : i + HEAD]
    return total


def attend_part(qb, keys, values, tile=2048):
    acc = sums = None
    for k_ref, v_ref in zip(keys, values):
        for i in range(0, 2048, tile):
            sc = lax.dot_general(
                qb, k_ref[i : i + tile, :], (((1,), (1,)), ((), ())), preferred_element_type=F32
            )
            e = jnp.exp2(sc)
            part = jnp.dot(e.astype(BF), v_ref[i : i + tile, :], preferred_element_type=F32)
            acc = part if acc is None else acc + part
            sums = lanes_summed(e) if sums is None else sums + lanes_summed(e)
    return acc, sums


def attend_own_kernel(*refs):
    q, k_ref, v_ref, acc_ref, sum_ref = refs[0:4], refs[4], refs[5], refs[6], refs[7]

    def head(h, _):
        at = pl.ds(pl.multiple_of(h * HEAD, HEAD), HEAD)
        for k in range(0, 4, 2):
            qb = jnp.concatenate([q[k][:, at], q[k + 1][:, at]], axis=0)
            to = pl.ds(pl.multiple_of(h * 1024 + k * 256, 256), 512)
            acc_ref[to], sum_ref[to] = attend_part(qb, [k_ref], [v_ref])
        return 0

    lax.fori_loop(0, 4, head, 0)


def attend_own(q, keys, values):
    return pl.pallas_call(
        attend_own_kernel,
        in_specs=[VMEM] * 6,
        out_specs=[VMEM, VMEM],
        out_shape=[jax.ShapeDtypeStruct((4096, HEAD), F32)] * 2,
        compiler_params=params(),
        cost_estimate=cost(4 * 4096 * 2048 * 256, 6 << 20, 4096 * 2048),
        name="attend_own",
    )(*q, keys, values)


def attend_heads_kernel(h, n, *refs):
    q, keys, values = refs[0:4], refs[4:8], refs[8:12]
    acc_ref, sum_ref, o_ref, qs, lowest = refs[12:]
    for i in range(n):
        for k in range(4):
            to = i * 1024 + k * 256
            qs[to : to + 256] = q[k][:, (h + i) * HEAD : (h + i + 1) * HEAD]
    lowest[...] = jnp.ones((8, HEAD), F32)

    def rows_of(i, _):
        at = pl.ds(pl.multiple_of(i * ROWS, ROWS), ROWS)
        acc, sums = attend_part(qs[at], keys[1:], values[1:])
        total = jnp.sum(sums + sum_ref[at], axis=1, keepdims=True)
        o_ref[at] = ((acc + acc_ref[at]) / total).astype(BF)
        good = (total >= 2.0**-100) & (total <= 2.0**100)
        lowest[...] = jnp.minimum(lowest[...], jnp.min(good.astype(F32)))
        return 0

    lax.fori_loop(0, n * 1024 // ROWS, rows_of, 0)

    @pl.when(jnp.min(lowest[...]) < 0.5)
    def _():
        def again(i, _):
            own = pl.ds(pl.multiple_of(i * 256, 256), 256)
            rows = qs[own]
            top = jnp.full((256, 1), -3e38, F32)
            total, acc = jnp.zeros((256, 1), F32), jnp.zeros((256, HEAD), F32)
            for k_ref, v_ref in zip(keys, values):

                def step(i, carry, k_ref=k_ref, v_ref=v_ref):
                    top, total, acc = carry
                    at = pl.ds(pl.multiple_of(i * 512, 512), 512)
                    sc = lax.dot_general(
                        rows, k_ref[at, :], (((1,), (1,)), ((), ())), preferred_element_type=F32
                    )
                    new = jnp.maximum(top, jnp.max(sc, axis=1, keepdims=True))
                    e, old = jnp.exp2(sc - new), jnp.exp2(top - new)
                    acc = acc * old + jnp.dot(e.astype(BF), v_ref[at, :], preferred_element_type=F32)
                    return new, total * old + jnp.sum(e, axis=1, keepdims=True), acc

                top, total, acc = lax.fori_loop(0, 4, step, (top, total, acc))
            o_ref[own] = (acc / total).astype(BF)
            return 0

        lax.fori_loop(0, n * 4, again, 0)


def attend_heads(h, n, q, keys, values, acc, sums):
    whole = lambda shape: pl.BlockSpec(shape, lambda i: (0,) * len(shape))
    some = pl.BlockSpec((n * 1024, HEAD), lambda i: (h // n, 0))
    return pl.pallas_call(
        functools.partial(attend_heads_kernel, h, n),
        grid=(1,),
        in_specs=[whole((256, 512))] * 4 + [whole((2048, HEAD))] * 8 + [some, some],
        out_specs=whole((n * 1024, HEAD)),
        out_shape=jax.ShapeDtypeStruct((n * 1024, HEAD), BF),
        scratch_shapes=[pltpu.VMEM((n * 1024, HEAD), BF), pltpu.VMEM((8, HEAD), F32)],
        compiler_params=params(),
        cost_estimate=cost(4 * n * 1024 * 6144 * 256, 6 << 20, n * 1024 * 6144),
        name=f"attend_heads{h}",
    )(*q, *keys, *values, acc, sums)


def project_kernel(first, sizes, place, *refs):
    n, count = sum(sizes), 4 * len(sizes)
    att = [(refs[4 * g : 4 * g + 4], i * 1024) for g, size in enumerate(sizes) for i in range(size)]
    own, oth = refs[count : count + 2]
    before = None if first == 0 else refs[count + 2]
    outs = refs[count + 2 + (first > 0) :]
    z = place[3]
    for half, w in enumerate((own, oth)):
        cols = slice(half * 512, (half + 1) * 512)
        rhs = []
        for j in range(4):
            row = pl.multiple_of(lax.rem(z + 4 - j, 4) * 512 + first * HEAD, HEAD)
            rhs.append(
                jnp.concatenate([w[m, pl.ds(row, n * HEAD), :] for m in range(4)], axis=1)
            )
        rhs = jnp.concatenate(rhs, axis=0)
        lhs = []
        for k in range(4):
            rows = [(k - j) % 4 * 256 for j in range(4)]
            lhs.append(
                jnp.concatenate(
                    [
                        ref[j][skip + rows[j] : skip + rows[j] + 256, :]
                        for j in range(4)
                        for ref, skip in att
                    ],
                    axis=1,
                )
            )
        total = jnp.dot(jnp.concatenate(lhs, axis=0), rhs, preferred_element_type=F32)
        if before is None:
            outs[0][:, cols] = total
        else:
            total = total + before[:, cols]
            for k in range(4):
                outs[k][:, cols] = total[k * 256 : k * 256 + 256].astype(BF)


def project(first, place, att, own, oth, before=None):
    last, sizes = before is not None, [group[0].shape[0] // 1024 for group in att]
    n = sum(sizes)
    return pl.pallas_call(
        functools.partial(project_kernel, first, sizes),
        in_specs=[SMEM] + [VMEM] * (4 * len(att) + 2 + last),
        out_specs=[VMEM] * (4 if last else 1),
        out_shape=[jax.ShapeDtypeStruct((256, 1024), BF)] * 4
        if last
        else [jax.ShapeDtypeStruct((1024, 1024), F32)],
        compiler_params=params(),
        cost_estimate=cost(1024 * 1024 * n * 1024, 10 << 20),
        name=f"project{first}",
    )(place, *[a for head in att for a in head], own, oth, *([before] if last else []))


def residual_kernel(place, acts, *refs):
    branch, o_ref = refs[0:4], refs[4]
    xl, y, z = place[1], place[2], place[3]
    for k in range(4):
        for half in range(2):
            b = xl if half == 0 else 1 - xl
            for m in range(4):
                block = b * 16 + lax.rem(y + 4 - m, 4) * 4 + lax.rem(z + k, 4)
                at = pl.ds(pl.multiple_of(block * 128, 128), 128)
                i = (half * 4 + m) * 128
                o_ref[:, at] = (acts[:, at].astype(F32) + branch[k][:, i : i + 128].astype(F32)).astype(BF)


def residual(place, acts, branch):
    return pl.pallas_call(
        residual_kernel,
        grid=(4,),
        in_specs=[SMEM, pl.BlockSpec((64, 4096), lambda i: (i, 0))]
        + [pl.BlockSpec((64, 1024), lambda i: (i, 0))] * 4,
        out_specs=pl.BlockSpec((64, 4096), lambda i: (i, 0)),
        out_shape=jax.ShapeDtypeStruct((256, 4096), BF),
        compiler_params=params(),
        cost_estimate=cost(256 * 4096, 6 << 20),
        name="residual",
    )(place, acts, *branch)


def tables(seq_index):
    freqs = ROPE_BASE ** (-2.0 * jnp.arange(HEAD // 2, dtype=F32) / HEAD)
    positions = seq_index * 256 + jnp.arange(256, dtype=jnp.int32)
    angles = positions.astype(F32)[:, None] * freqs[None, :]
    cosine, sine = jnp.cos(angles), jnp.sin(angles)
    return jnp.concatenate([cosine, cosine], 1), jnp.concatenate([-sine, sine], 1)


def turn(xh, c, b, y, z, flip=0):
    return xh, b ^ flip, c, y, z


def after(x, *ready):
    return lax.optimization_barrier((x, *ready))[0]


def body(acts, norm_gain, w_query, w_key, w_value, w_out):
    section, seq = lax.axis_index("section"), lax.axis_index("seq")
    core, xl, y, z = section % 2, seq // 16, seq // 4 % 4, seq % 4
    place = jnp.stack([core, xl, y, z]).astype(jnp.int32)
    tokens = acts[0]
    low = xl == 0
    mine, cross = jnp.where(low, w_key[0], w_value[0]), jnp.where(low, w_value[0], w_key[0])
    first = [send(mine, lambda xh, c, b, y, z, m=m: turn(xh, c, b, y + m, z)) for m in range(4)]
    second = [send(cross, lambda xh, c, b, y, z, j=j: turn(xh, c, b, y, z + j, 1)) for j in range(4)]
    floats = tokens.astype(F32)
    normed = (
        floats * lax.rsqrt(jnp.mean(floats * floats, axis=-1, keepdims=True) + EPS) * norm_gain[0]
    ).astype(BF)
    own = send(after(normed, *first, *second), turn)
    first, second = jnp.concatenate(first, 0), jnp.concatenate(second, 0)

    cos_n, sin_n = tables(seq)
    q = queries(place, after(normed, first, second), w_query, cos_n, sin_n)
    firsts = {j: along_z(first, j) for j in (1, 3)}
    seconds = {m: along_y(second, m) for m in (1, 3)}
    near = firsts[1], firsts[3], seconds[1], seconds[3]
    firsts[2], seconds[2] = along_z(after(first, *q), 2), along_y(after(second, *q), 2)
    firsts = [first] + [firsts[j] for j in (1, 2, 3)]
    seconds = [second] + [seconds[m] for m in (1, 2, 3)]
    other = swap_core(after(own, *near, *q))
    q = [
        send(after(q[k], firsts[2], seconds[2]), lambda xh, c, b, y, z, k=k: turn(xh, c, b, y, z + k)) for k in range(4)
    ]

    is_key = core == 0
    rope = [tables(b * 16 + y * 4 + z) for b in (core, 1 - core)]
    cos_k = jnp.where(is_key, jnp.stack([t[0] for t in rope]), 1.0)
    sin_k = jnp.where(is_key, jnp.stack([t[1] for t in rope]), 0.0)
    kv = keys_or_values(place, own, other, cos_k, sin_k, firsts, seconds)
    kv = jnp.concatenate([kv[0]] + [along_z(kv[k], k) for k in (1, 2, 3)], 0)
    mine = [kv] + [along_y(kv, m) for m in (1, 2, 3)]
    theirs = [swap_core(kv)]
    def in_order(a, b):
        return jnp.where(is_key, a, b), jnp.where(is_key, b, a)

    pairs = [in_order(mine[0], theirs[0])]
    acc, sums = attend_own(q, *pairs[0])
    theirs += [swap_core(after(mine[m], acc)) for m in (1, 2, 3)]
    pairs += [in_order(mine[m], theirs[m]) for m in (1, 2, 3)]
    keys, values = zip(*pairs)
    w_own = send(after(w_out[0], kv), turn)
    passed = send(after(tokens, theirs[0]), onward)
    w_send = after(w_own, *theirs)
    w_all = [w_own, along_y(w_send, 1), None, along_y(w_send, 3)]
    heads = []
    for h, n in GROUPS:
        att = attend_heads(h, n, q, keys, values, acc, sums)
        out = after(att, *heads[-1][1:]) if heads else att
        heads.append([att] + [along_z(out, j) for j in (1, 2, 3)])
        if len(heads) == 1:
            w_all[2] = along_y(after(w_own, w_all[1], w_all[3], att), 2)
        if len(heads) == 2:
            w_own = jnp.stack([after(w, att, *heads[0][1:]) for w in w_all])
            w_other = swap_core(w_own)
        ready = [att] + (heads[-2][1:] if heads[1:] else [])
        acc, sums = after(acc, *ready), after(sums, *ready)
    heads[0][0] = after(heads[0][0], att, passed)
    branch = project(0, place, heads[:-1], w_own, w_other)[0]
    branch = project(GROUPS[-1][0], place, heads[-1:], w_own, w_other, branch)

    def home(k):
        def move(xh, c, b, y, z):
            s = (2 * xh + b + 1) % 4
            return s // 2, s % 2, c, y, z - k

        return move

    branch = [send(branch[k], home(k)) for k in range(4)]
    return residual(place, passed, branch)[None]


def onward(xh, c, b, y, z):
    s = (2 * xh + c + 1) % 4
    return s // 2, s % 2, b, y, z


def solution(mesh):
    return jax.shard_map(
        body,
        mesh=mesh,
        in_specs=(
            P("section", "seq", None),
            P("section", None),
            P("section", None, None),
            P("section", "seq", None),
            P("section", "seq", None),
            P("section", None, "seq"),
        ),
        out_specs=P("section", "seq", None),
        check_vma=False,
    )
```

```python
import functools
import math

import jax
import jax.numpy as jnp
from jax import lax
from jax.experimental import pallas as pl
from jax.experimental.pallas import tpu as pltpu
from jax.sharding import PartitionSpec as P

HEAD = 128
EPS = 1e-05
ROPE_BASE = 500000.0
SEQ = 32
BF = jnp.bfloat16
F32 = jnp.float32
VMEM = pl.BlockSpec(memory_space=pltpu.VMEM)
SMEM = pl.BlockSpec(memory_space=pltpu.SMEM)
ROWS = 1024
GROUPS = ((0, 2), (2, 2))
Q_FOLD = math.log2(math.e) / math.sqrt(HEAD)


def send(x, move):
    pairs = []
    for s in range(4):
        for d in range(SEQ):
            xh, core, xl, y, z = move(s // 2, s % 2, d // 16, d // 4 % 4, d % 4)
            pairs.append((s * SEQ + d, (xh * 2 + core) * SEQ + xl * 16 + y % 4 * 4 + z % 4))
    return lax.ppermute(x, ("section", "seq"), pairs)


def along_y(x, k):
    return send(x, lambda xh, c, b, y, z: (xh, c, b, y + k, z))


def along_z(x, k):
    return send(x, lambda xh, c, b, y, z: (xh, c, b, y, z + k))


def swap_core(x):
    return send(x, lambda xh, c, b, y, z: (xh, 1 - c, b, y, z))


def params(**kw):
    return pltpu.CompilerParams(vmem_limit_bytes=36 * 1024 * 1024, **kw)


def cost(flops, nbytes, transcendentals=0):
    return pl.CostEstimate(flops=flops, bytes_accessed=nbytes, transcendentals=transcendentals)


def query_kernel(place, x_ref, w_ref, c_ref, s_ref, *outs):
    u = jnp.dot(x_ref[...], w_ref[0], preferred_element_type=F32)
    done = []
    for h in range(4):
        v = u[:, h * HEAD : (h + 1) * HEAD]
        done.append(((v * c_ref[...] + pltpu.roll(v, 64, 1) * s_ref[...]) * Q_FOLD).astype(BF))
    done = jnp.concatenate(done, axis=1)
    for k in range(4):

        @pl.when(pl.program_id(0) == k)
        def _(k=k):
            outs[k][...] = done


def queries(place, x, w, c, s):
    return pl.pallas_call(
        query_kernel,
        grid_spec=pltpu.PrefetchScalarGridSpec(
            num_scalar_prefetch=1,
            grid=(4,),
            in_specs=[
                pl.BlockSpec((256, 4096), lambda k, p: (0, 0)),
                pl.BlockSpec((1, 4096, 512), lambda k, p: (0, 0, lax.rem(p[3] + k, 4))),
                pl.BlockSpec((256, HEAD), lambda k, p: (0, 0)),
                pl.BlockSpec((256, HEAD), lambda k, p: (0, 0)),
            ],
            out_specs=[pl.BlockSpec((256, 512), lambda k, p: (0, 0))] * 4,
        ),
        out_shape=[jax.ShapeDtypeStruct((256, 512), BF)] * 4,
        compiler_params=params(),
        cost_estimate=cost(2 * 256 * 4096 * 2048, 20 << 20),
        name="queries",
    )(place, x, w, c, s)


def kv_kernel(place, own, oth, c_ref, s_ref, *rest):
    first, second = rest[0:4], rest[4:8]
    outs, acc = rest[8:12], rest[12]
    core, y, z = place[0], place[2], place[3]

    def columns(ref, blocks):
        return jnp.concatenate(
            [ref[:, pl.ds(pl.multiple_of(b * 128, 128), 128)] for b in blocks], axis=1
        )

    for which in range(8):
        if which < 4:
            w = first[which]
            blocks = [core * 16 + lax.rem(y + 4 - m, 4) * 4 + lax.rem(z + 4 - which, 4) for m in range(4)]
        else:
            w = second[which - 4]
            blocks = [
                (1 - core) * 16 + lax.rem(y + 8 - which, 4) * 4 + lax.rem(z + 4 - j, 4)
                for j in range(4)
            ]
        x = jnp.concatenate([columns(own, blocks), columns(oth, blocks)], axis=0)
        part = jnp.dot(x, w[...], preferred_element_type=F32)
        if which == 0:
            acc[...] = part
        else:
            acc[...] += part
    for t in range(2):
        row = pl.multiple_of(lax.select(t == 0, core, 1 - core) * 256, 256)
        for k in range(4):
            v = acc[t * 256 : t * 256 + 256, pl.ds(pl.multiple_of(lax.rem(z + k, 4) * HEAD, HEAD), HEAD)]
            rows = v * c_ref[t] + pltpu.roll(v, 64, 1) * s_ref[t]
            outs[k][pl.ds(row, 256), :] = rows.astype(BF)


def keys_or_values(place, own, oth, c, s, first, second):
    return pl.pallas_call(
        kv_kernel,
        in_specs=[SMEM] + [VMEM] * 12,
        out_specs=[VMEM] * 4,
        out_shape=[jax.ShapeDtypeStruct((512, HEAD), BF)] * 4,
        scratch_shapes=[pltpu.VMEM((512, 512), F32)],
        compiler_params=params(),
        cost_estimate=cost(2 * 512 * 4096 * 512, 9 << 20),
        name="keys_or_values",
    )(place, own, oth, c, s, *first, *second)


def lanes_summed(e):
    total = e[:, :HEAD]
    for i in range(HEAD, e.shape[1], HEAD):
        total = total + e[:, i : i + HEAD]
    return total


def attend_part(qb, keys, values, tile=2048):
    acc = sums = None
    for k_ref, v_ref in zip(keys, values):
        for i in range(0, 2048, tile):
            sc = lax.dot_general(
                qb, k_ref[i : i + tile, :], (((1,), (1,)), ((), ())), preferred_element_type=F32
            )
            e = jnp.exp2(sc)
            part = jnp.dot(e.astype(BF), v_ref[i : i + tile, :], preferred_element_type=F32)
            acc = part if acc is None else acc + part
            sums = lanes_summed(e) if sums is None else sums + lanes_summed(e)
    return acc, sums


def attend_own_kernel(*refs):
    q, k_ref, v_ref, acc_ref, sum_ref = refs[0:4], refs[4], refs[5], refs[6], refs[7]

    def head(h, _):
        at = pl.ds(pl.multiple_of(h * HEAD, HEAD), HEAD)
        for k in range(0, 4, 2):
            qb = jnp.concatenate([q[k][:, at], q[k + 1][:, at]], axis=0)
            to = pl.ds(pl.multiple_of(h * 1024 + k * 256, 256), 512)
            acc_ref[to], sum_ref[to] = attend_part(qb, [k_ref], [v_ref])
        return 0

    lax.fori_loop(0, 4, head, 0)


def attend_own(q, keys, values):
    return pl.pallas_call(
        attend_own_kernel,
        in_specs=[VMEM] * 6,
        out_specs=[VMEM, VMEM],
        out_shape=[jax.ShapeDtypeStruct((4096, HEAD), F32)] * 2,
        compiler_params=params(),
        cost_estimate=cost(4 * 4096 * 2048 * 256, 6 << 20, 4096 * 2048),
        name="attend_own",
    )(*q, keys, values)


def attend_heads_kernel(h, n, *refs):
    q, keys, values = refs[0:4], refs[4:8], refs[8:12]
    acc_ref, sum_ref, o_ref, qs, lowest = refs[12:]
    for i in range(n):
        for k in range(4):
            to = i * 1024 + k * 256
            qs[to : to + 256] = q[k][:, (h + i) * HEAD : (h + i + 1) * HEAD]
    lowest[...] = jnp.ones((8, HEAD), F32)

    def rows_of(i, _):
        at = pl.ds(pl.multiple_of(i * ROWS, ROWS), ROWS)
        acc, sums = attend_part(qs[at], keys[1:], values[1:])
        total = jnp.sum(sums + sum_ref[at], axis=1, keepdims=True)
        o_ref[at] = ((acc + acc_ref[at]) / total).astype(BF)
        good = (total >= 2.0**-100) & (total <= 2.0**100)
        lowest[...] = jnp.minimum(lowest[...], jnp.min(good.astype(F32)))
        return 0

    lax.fori_loop(0, n * 1024 // ROWS, rows_of, 0)

    @pl.when(jnp.min(lowest[...]) < 0.5)
    def _():
        def again(i, _):
            own = pl.ds(pl.multiple_of(i * 256, 256), 256)
            rows = qs[own]
            top = jnp.full((256, 1), -3e38, F32)
            total, acc = jnp.zeros((256, 1), F32), jnp.zeros((256, HEAD), F32)
            for k_ref, v_ref in zip(keys, values):

                def step(i, carry, k_ref=k_ref, v_ref=v_ref):
                    top, total, acc = carry
                    at = pl.ds(pl.multiple_of(i * 512, 512), 512)
                    sc = lax.dot_general(
                        rows, k_ref[at, :], (((1,), (1,)), ((), ())), preferred_element_type=F32
                    )
                    new = jnp.maximum(top, jnp.max(sc, axis=1, keepdims=True))
                    e, old = jnp.exp2(sc - new), jnp.exp2(top - new)
                    acc = acc * old + jnp.dot(e.astype(BF), v_ref[at, :], preferred_element_type=F32)
                    return new, total * old + jnp.sum(e, axis=1, keepdims=True), acc

                top, total, acc = lax.fori_loop(0, 4, step, (top, total, acc))
            o_ref[own] = (acc / total).astype(BF)
            return 0

        lax.fori_loop(0, n * 4, again, 0)


def attend_heads(h, n, q, keys, values, acc, sums):
    whole = lambda shape: pl.BlockSpec(shape, lambda i: (0,) * len(shape))
    some = pl.BlockSpec((n * 1024, HEAD), lambda i: (h // n, 0))
    return pl.pallas_call(
        functools.partial(attend_heads_kernel, h, n),
        grid=(1,),
        in_specs=[whole((256, 512))] * 4 + [whole((2048, HEAD))] * 8 + [some, some],
        out_specs=whole((n * 1024, HEAD)),
        out_shape=jax.ShapeDtypeStruct((n * 1024, HEAD), BF),
        scratch_shapes=[pltpu.VMEM((n * 1024, HEAD), BF), pltpu.VMEM((8, HEAD), F32)],
        compiler_params=params(),
        cost_estimate=cost(4 * n * 1024 * 6144 * 256, 6 << 20, n * 1024 * 6144),
        name=f"attend_heads{h}",
    )(*q, *keys, *values, acc, sums)


def project_kernel(first, sizes, place, *refs):
    n, count = sum(sizes), 4 * len(sizes)
    att = [(refs[4 * g : 4 * g + 4], i * 1024) for g, size in enumerate(sizes) for i in range(size)]
    own, oth = refs[count : count + 2]
    before = None if first == 0 else refs[count + 2]
    outs = refs[count + 2 + (first > 0) :]
    z = place[3]
    for half, w in enumerate((own, oth)):
        cols = slice(half * 512, (half + 1) * 512)
        rhs = []
        for j in range(4):
            row = pl.multiple_of(lax.rem(z + 4 - j, 4) * 512 + first * HEAD, HEAD)
            rhs.append(
                jnp.concatenate([w[m, pl.ds(row, n * HEAD), :] for m in range(4)], axis=1)
            )
        rhs = jnp.concatenate(rhs, axis=0)
        lhs = []
        for k in range(4):
            rows = [(k - j) % 4 * 256 for j in range(4)]
            lhs.append(
                jnp.concatenate(
                    [
                        ref[j][skip + rows[j] : skip + rows[j] + 256, :]
                        for j in range(4)
                        for ref, skip in att
                    ],
                    axis=1,
                )
            )
        total = jnp.dot(jnp.concatenate(lhs, axis=0), rhs, preferred_element_type=F32)
        if before is None:
            outs[0][:, cols] = total
        else:
            total = total + before[:, cols]
            for k in range(4):
                outs[k][:, cols] = total[k * 256 : k * 256 + 256].astype(BF)


def project(first, place, att, own, oth, before=None):
    last, sizes = before is not None, [group[0].shape[0] // 1024 for group in att]
    n = sum(sizes)
    return pl.pallas_call(
        functools.partial(project_kernel, first, sizes),
        in_specs=[SMEM] + [VMEM] * (4 * len(att) + 2 + last),
        out_specs=[VMEM] * (4 if last else 1),
        out_shape=[jax.ShapeDtypeStruct((256, 1024), BF)] * 4
        if last
        else [jax.ShapeDtypeStruct((1024, 1024), F32)],
        compiler_params=params(),
        cost_estimate=cost(1024 * 1024 * n * 1024, 10 << 20),
        name=f"project{first}",
    )(place, *[a for head in att for a in head], own, oth, *([before] if last else []))


def residual_kernel(place, acts, *refs):
    branch, o_ref = refs[0:4], refs[4]
    xl, y, z = place[1], place[2], place[3]
    for k in range(4):
        for half in range(2):
            b = xl if half == 0 else 1 - xl
            for m in range(4):
                block = b * 16 + lax.rem(y + 4 - m, 4) * 4 + lax.rem(z + k, 4)
                at = pl.ds(pl.multiple_of(block * 128, 128), 128)
                i = (half * 4 + m) * 128
                o_ref[:, at] = (acts[:, at].astype(F32) + branch[k][:, i : i + 128].astype(F32)).astype(BF)


def residual(place, acts, branch):
    return pl.pallas_call(
        residual_kernel,
        grid=(4,),
        in_specs=[SMEM, pl.BlockSpec((64, 4096), lambda i: (i, 0))]
        + [pl.BlockSpec((64, 1024), lambda i: (i, 0))] * 4,
        out_specs=pl.BlockSpec((64, 4096), lambda i: (i, 0)),
        out_shape=jax.ShapeDtypeStruct((256, 4096), BF),
        compiler_params=params(),
        cost_estimate=cost(256 * 4096, 6 << 20),
        name="residual",
    )(place, acts, *branch)


def tables(seq_index):
    freqs = ROPE_BASE ** (-2.0 * jnp.arange(HEAD // 2, dtype=F32) / HEAD)
    positions = seq_index * 256 + jnp.arange(256, dtype=jnp.int32)
    angles = positions.astype(F32)[:, None] * freqs[None, :]
    cosine, sine = jnp.cos(angles), jnp.sin(angles)
    return jnp.concatenate([cosine, cosine], 1), jnp.concatenate([-sine, sine], 1)


def turn(xh, c, b, y, z, flip=0):
    return xh, b ^ flip, c, y, z


def after(x, *ready):
    return lax.optimization_barrier((x, *ready))[0]


def body(acts, norm_gain, w_query, w_key, w_value, w_out):
    section, seq = lax.axis_index("section"), lax.axis_index("seq")
    core, xl, y, z = section % 2, seq // 16, seq // 4 % 4, seq % 4
    place = jnp.stack([core, xl, y, z]).astype(jnp.int32)
    tokens = acts[0]
    low = xl == 0
    mine, cross = jnp.where(low, w_key[0], w_value[0]), jnp.where(low, w_value[0], w_key[0])
    first = [send(mine, lambda xh, c, b, y, z, m=m: turn(xh, c, b, y + m, z)) for m in range(4)]
    second = [send(cross, lambda xh, c, b, y, z, j=j: turn(xh, c, b, y, z + j, 1)) for j in range(4)]
    floats = tokens.astype(F32)
    normed = (
        floats * lax.rsqrt(jnp.mean(floats * floats, axis=-1, keepdims=True) + EPS) * norm_gain[0]
    ).astype(BF)
    own = send(after(normed, *first, *second), turn)
    first, second = jnp.concatenate(first, 0), jnp.concatenate(second, 0)

    cos_n, sin_n = tables(seq)
    q = queries(place, after(normed, first, second), w_query, cos_n, sin_n)
    firsts = {j: along_z(first, j) for j in (1, 3)}
    seconds = {m: along_y(second, m) for m in (1, 3)}
    near = firsts[1], firsts[3], seconds[1], seconds[3]
    firsts[2], seconds[2] = along_z(after(first, *q), 2), along_y(after(second, *q), 2)
    firsts = [first] + [firsts[j] for j in (1, 2, 3)]
    seconds = [second] + [seconds[m] for m in (1, 2, 3)]
    other = swap_core(after(own, *near, *q))
    q = [
        send(after(q[k], firsts[2], seconds[2]), lambda xh, c, b, y, z, k=k: turn(xh, c, b, y, z + k)) for k in range(4)
    ]

    is_key = core == 0
    rope = [tables(b * 16 + y * 4 + z) for b in (core, 1 - core)]
    cos_k = jnp.where(is_key, jnp.stack([t[0] for t in rope]), 1.0)
    sin_k = jnp.where(is_key, jnp.stack([t[1] for t in rope]), 0.0)
    kv = keys_or_values(place, own, other, cos_k, sin_k, firsts, seconds)
    kv = jnp.concatenate([kv[0]] + [along_z(kv[k], k) for k in (1, 2, 3)], 0)
    mine = [kv] + [along_y(kv, m) for m in (1, 2, 3)]
    theirs = [swap_core(kv)]
    def in_order(a, b):
        return jnp.where(is_key, a, b), jnp.where(is_key, b, a)

    pairs = [in_order(mine[0], theirs[0])]
    acc, sums = attend_own(q, *pairs[0])
    theirs += [swap_core(after(mine[m], acc)) for m in (1, 2, 3)]
    pairs += [in_order(mine[m], theirs[m]) for m in (1, 2, 3)]
    keys, values = zip(*pairs)
    w_own = send(after(w_out[0], kv), turn)
    passed = send(after(tokens, theirs[0]), onward)
    w_send = after(w_own, *theirs)
    w_all = [w_own, along_y(w_send, 1), None, along_y(w_send, 3)]
    heads = []
    for h, n in GROUPS:
        att = attend_heads(h, n, q, keys, values, acc, sums)
        out = after(att, *heads[-1][1:]) if heads else att
        heads.append([att] + [along_z(out, j) for j in (1, 2, 3)])
        if len(heads) == 1:
            w_all[2] = along_y(after(w_own, w_all[1], w_all[3], att), 2)
        if len(heads) == 2:
            w_own = jnp.stack([after(w, att, *heads[0][1:]) for w in w_all])
            w_other = swap_core(w_own)
        ready = [att] + (heads[-2][1:] if heads[1:] else [])
        acc, sums = after(acc, *ready), after(sums, *ready)
    heads[0][0] = after(heads[0][0], att, passed)
    branch = project(0, place, heads[:-1], w_own, w_other)[0]
    branch = project(GROUPS[-1][0], place, heads[-1:], w_own, w_other, branch)

    def home(k):
        def move(xh, c, b, y, z):
            s = (2 * xh + b + 1) % 4
            return s // 2, s % 2, c, y, z - k

        return move

    branch = [send(branch[k], home(k)) for k in range(4)]
    return residual(place, passed, branch)[None]


def onward(xh, c, b, y, z):
    s = (2 * xh + c + 1) % 4
    return s // 2, s % 2, b, y, z


def solution(mesh):
    return jax.shard_map(
        body,
        mesh=mesh,
        in_specs=(
            P("section", "seq", None),
            P("section", None),
            P("section", None, None),
            P("section", "seq", None),
            P("section", "seq", None),
            P("section", None, "seq"),
        ),
        out_specs=P("section", "seq", None),
        check_vma=False,
    )
```
